512 devices in a mesh: seq: 64 (over y, z_hi, x), head: 8 (over z_lo, core).
Axes of the slice: x: 4, y: 8, z: 8 (z_hi: 2, z_lo: 4; z = z_hi * 4 + z_lo), core: 2. Of those that a mesh axis runs over, the one named last changes fastest.
Arguments:
- q_proj: bfloat16 [49152, 5120], P('seq', 'head'), may hold values from -500 to 500
- k_proj: bfloat16 [49152, 5120], P('seq', 'head'), may hold values from -500 to 500
- v_proj: bfloat16 [49152, 5120], P('seq', 'head'), may hold values from -6 to 6
- q_gain: float32 [5120], P('head'), may hold values from 0.25 to 1.75
- k_gain: float32 [5120], P('head'), may hold values from 0.25 to 1.75
- window_tiles: int32 [40, 128, 3], P('head'), may hold values from -2 to 127, as said below
- window_count: int32 [40, 128], P('head'), may hold values from 1 to 3
Outputs:
- attended: bfloat16 [49152, 5120], P('seq', 'head')
The draws below stay inside these ranges and needn't reach their ends.
Inputs may be any that keep to these rules, and one draw needn't show every extreme that they name: Entry 0 of window_tiles[h, t] is t; the other entries are distinct tiles t - o with 1 <= o <= 2; negative entries are never seen.
All inputs are finite; a program needn't handle non-finite values.
Results may differ from the reference program's by a relative error of at most 0.012.
Values may be sent and summed in bfloat16 or wider, within the bound.
A program may use at most 64 MiB of HBM per device.

```python
import math
import jax
import jax.numpy as jnp
from jax import lax

D = 5120
HEADS = 40
HEAD_DIM = 128
TILE = 384
SPAN = 2
WIN = 3
TOKENS = 49152
NTILES = 128


def window_pair(key):
    folded = jax.random.fold_in(key, 11)
    first_key, second_key = jax.random.split(folded)
    ranks = jax.random.randint(first_key, (HEADS, NTILES, SPAN), 0, 1 << 20) * SPAN + jnp.arange(SPAN)[None, None, :]
    order = jnp.argsort(ranks, axis=-1, stable=True)
    offsets = order[:, :, :WIN - 1] + 1
    tile_ids = jnp.broadcast_to(jnp.arange(NTILES)[None, :, None], (HEADS, NTILES, 1))
    tiles = jnp.concatenate([tile_ids, tile_ids - offsets], axis=-1).astype(jnp.int32)
    counts = jax.random.randint(second_key, (HEADS, NTILES), 1, WIN + 1)
    last_tile = jnp.arange(NTILES)[None, :] == NTILES - 1
    counts = jnp.where(last_tile, WIN, counts).astype(jnp.int32)
    return (tiles, counts)


def draw_window_tiles(key, part):
    return window_pair(key)[0]


def draw_window_count(key, part):
    return window_pair(key)[1]


def query_key_pair(key):
    folded = jax.random.fold_in(key, 23)
    keys = jax.random.split(folded, 4)
    column = jnp.arange(D, dtype=jnp.float32) / (D - 1)
    ln_ten = math.log(10.0)
    row_q = jnp.exp(jax.random.uniform(keys[0], (TOKENS, 1), jnp.float32, 0.0, ln_ten))
    row_k = jnp.exp(jax.random.uniform(keys[1], (TOKENS, 1), jnp.float32, 0.0, ln_ten))
    col_scale = jnp.exp(column * ln_ten)[None, :]
    base_q = jnp.clip(jax.random.normal(keys[2], (TOKENS, D), jnp.float32), -4.0, 4.0)
    base_k = jnp.clip(jax.random.normal(keys[3], (TOKENS, D), jnp.float32), -4.0, 4.0)
    queries = base_q * row_q * col_scale
    keyset = base_k * row_k * col_scale
    return (queries, keyset)


def draw_q_proj(key, part):
    return query_key_pair(key)[0].astype(jnp.bfloat16)


def draw_k_proj(key, part):
    return query_key_pair(key)[1].astype(jnp.bfloat16)


def block_levels(stream_key, extent, pieces, low, top_value):
    loudness, own = 1.0, jax.random.fold_in(stream_key, 6)
    for position, parts in pieces:
        steps = jnp.exp(jax.random.uniform(jax.random.fold_in(own, position), (parts,), jnp.float32, low / len(pieces), top_value / len(pieces)))
        loudness = loudness * jnp.repeat(steps, extent[position] // parts).reshape([-1 if axis == position else 1 for axis in range(len(extent))])
    return loudness


def noise(stream_key, extent, spread, reach, shards=(), kind=jnp.bfloat16):
    drawn = spread * jax.random.normal(stream_key, extent, jnp.float32)
    if shards:
        drawn = drawn * block_levels(stream_key, extent, shards, -0.22, 0.18)
    return jnp.clip(drawn, -reach, reach).astype(kind)


def setup_inputs(seed: int = 0) -> dict:
    splits = jax.random.split(jax.random.key(seed), 8)
    q_proj = draw_q_proj(jax.random.fold_in(splits[7], 71), 0)
    k_proj = draw_k_proj(jax.random.fold_in(splits[7], 71), 0)
    v_proj = noise(splits[2], (TOKENS, D), 1.0, 6.0, ((0, 64), (1, 8)))
    q_gain = jnp.clip(1.0 + 0.15 * jax.random.normal(splits[3], (D,), jnp.float32), 0.25, 1.75)
    k_gain = jnp.clip(1.0 + 0.15 * jax.random.normal(splits[4], (D,), jnp.float32), 0.25, 1.75)
    window_tiles = draw_window_tiles(jax.random.fold_in(splits[7], 71), 0)
    window_count = draw_window_count(jax.random.fold_in(splits[7], 71), 0)
    return {"q_proj": q_proj, "k_proj": k_proj, "v_proj": v_proj, "q_gain": q_gain, "k_gain": k_gain, "window_tiles": window_tiles, "window_count": window_count}


NORM_EPS = 1e-06

def normalize(values, gain_vec):
    wide = values.astype(jnp.float32)
    row_total = lax.optimization_barrier(jnp.sum(wide * wide, axis=1, keepdims=True))
    return (wide * lax.rsqrt(row_total / D + NORM_EPS) * gain_vec[None, :]).astype(jnp.bfloat16)

def reference(q_proj, k_proj, v_proj, q_gain, k_gain, window_tiles, window_count):
    tile_total = TOKENS // TILE
    scale = HEAD_DIM ** (-0.5)
    q_all = normalize(q_proj, q_gain)
    k_all = normalize(k_proj, k_gain)

    def heads_major(values):
        return values.reshape(tile_total, TILE, HEADS, HEAD_DIM).transpose(2, 0, 1, 3)

    def one_head(per_head):
        q_heads, k_heads, v_heads, tiles, counts = per_head
        active = (jnp.arange(WIN)[None, :] < counts[:, None]) & (tiles >= 0)
        tile_index = jnp.clip(tiles, 0, tile_total - 1).astype(jnp.int32)
        k_taken = k_heads[tile_index].reshape(tile_total, WIN * TILE, HEAD_DIM)
        v_taken = v_heads[tile_index].reshape(tile_total, WIN * TILE, HEAD_DIM)
        scores = jnp.einsum('tqd,txd->tqx', q_heads.astype(jnp.float32), k_taken.astype(jnp.float32)) * scale
        key_mask = jnp.broadcast_to(active[:, None, :, None], (tile_total, 1, WIN, TILE)).reshape(tile_total, 1, WIN * TILE)
        scores = jnp.where(key_mask, scores, -jnp.inf)
        row_max = lax.optimization_barrier(jnp.max(scores, axis=-1, keepdims=True))
        exp_scores = jnp.where(key_mask, jnp.exp(scores - row_max), 0.0)
        weights_bf = (exp_scores / lax.optimization_barrier(jnp.sum(exp_scores, axis=-1, keepdims=True))).astype(jnp.bfloat16)
        result = jnp.einsum('tqx,txd->tqd', weights_bf.astype(jnp.float32), v_taken.astype(jnp.float32))
        return result.astype(jnp.bfloat16)
    outputs = lax.map(one_head, (heads_major(q_all), heads_major(k_all), heads_major(v_proj), window_tiles, window_count))
    return outputs.transpose(1, 2, 0, 3).reshape(TOKENS, D)
```

```python
import functools
import math

import jax
import jax.numpy as jnp
from jax import lax
from jax.experimental import pallas as pl
from jax.experimental.pallas import tpu as pltpu
from jax.sharding import PartitionSpec as P

HEAD_DIM = 128
WIN = 3
NORM_EPS = 1e-06
EXP_SCALE = math.log2(math.e) / math.sqrt(HEAD_DIM)
LOW = -1e30
HIGH = 1e30
F32 = jnp.float32
BF16 = jnp.bfloat16
MESH = pl.DeviceIdType.MESH


def dot_nt(a, b):
    return lax.dot_general(a, b, (((1,), (1,)), ((), ())), preferred_element_type=F32)


def dot_tn(a, b):
    return lax.dot_general(a, b, (((0,), (0,)), ((), ())), preferred_element_type=F32)


def routes(heads):
    units = 4 * heads
    via_two = [u for u in range(units - 2) if u % 3 == 0][: (units * 3) // 10]
    via_zero = [u for u in range(units) if u % 3 == 1]
    direct = [u for u in range(units) if u not in via_two and u not in via_zero]
    return via_two, via_zero, direct


def kernel(
    seqs,
    group,
    q_hbm,
    k_hbm,
    v_hbm,
    qg_ref,
    kg_ref,
    tiles_ref,
    count_ref,
    out_hbm,
    ql,
    kl,
    vl,
    halo,
    relay_buf,
    q_next,
    o_send,
    o_recv,
    ml_send,
    ml_recv,
    acc,
    ml,
    col_own,
    col_prev,
    col_next,
    stats,
    inv_own,
    inv_prev,
    inv_next,
    out_buf,
    load_sem,
    unit_send,
    unit_recv,
    relay_send,
    relay_recv,
    q_send_sem,
    q_recv_sem,
    o_send_sem,
    o_recv_sem,
    ml_sem,
    stat_send,
    stat_recv,
    inv_sem,
    out_sem,
):
    heads, rows, _ = ql.shape
    tile = rows // 2
    model = heads * HEAD_DIM * group
    units = 4 * heads
    via_two, via_zero, direct = routes(heads)
    s = lax.axis_index("seq")
    me = lax.axis_index("head")
    x = lax.rem(s, 4)
    first = s * 2

    def at(step):
        return {"seq": lax.rem(s + step + seqs, seqs), "head": me}

    def remote(src, dst, send, recv, where):
        return pltpu.make_async_remote_copy(
            src_ref=src, dst_ref=dst, send_sem=send, recv_sem=recv, device_id=where, device_id_type=MESH
        )

    def loads(which):
        src, dst = ((q_hbm, ql), (k_hbm, kl), (v_hbm, vl))[which]
        return [
            pltpu.make_async_copy(src.at[:, pl.ds(h * HEAD_DIM, HEAD_DIM)], dst.at[h], load_sem.at[which, h])
            for h in range(heads)
        ]

    for which in range(3):
        for copy in loads(which):
            copy.start()

    barrier = pltpu.get_barrier_semaphore()

    def greet(where):
        pl.semaphore_signal(barrier, inc=1, device_id=where, device_id_type=MESH)

    greet(at(1))
    greet(at(-1))

    @pl.when((x == 0) | (x == 2))
    def _():
        greet(at(3))

    @pl.when((x == 1) | (x == 3))
    def _():
        greet(at(-3))

    @pl.when(x == 0)
    def _():
        greet(at(4))
        greet(at(-4))

    for d in range(1, group):
        greet({"seq": s, "head": lax.rem(me + d, group)})

    ones = jnp.ones((8, HEAD_DIM), BF16)
    for which, buf in ((0, ql), (1, kl)):
        for copy in loads(which):
            copy.wait()

        def square_sum(h, total, buf=buf):
            wide = buf[h].astype(F32)
            sq = wide * wide
            hi = sq.astype(BF16)
            lo = (sq - hi.astype(F32)).astype(BF16)
            return total + dot_nt(ones, hi) + dot_nt(ones, lo)

        total = lax.fori_loop(0, heads, square_sum, jnp.zeros((8, rows), F32))
        stats[me, :, which * rows : (which + 1) * rows] = total[:1]

    @pl.when(x == 0)
    def _():
        pl.semaphore_wait(barrier, group - 1 + 5)

    @pl.when(x > 0)
    def _():
        pl.semaphore_wait(barrier, group - 1 + 3)

    def stat_copy(d):
        return remote(
            stats.at[me], stats.at[me], stat_send.at[d], stat_recv.at[me], {"seq": s, "head": lax.rem(me + d, group)}
        )

    for d in range(1, group):
        stat_copy(d).start()

    def unit_src(u):
        h, part = u // 4, u % 4
        src = v_hbm if part % 2 else k_hbm
        row = 0 if part >= 2 else tile
        return src.at[pl.ds(row, tile), pl.ds(h * HEAD_DIM, HEAD_DIM)]

    def near_copy(u):
        return remote(unit_src(u), halo.at[u], unit_send.at[u], unit_recv.at[u], at(1))

    def far_copy(u):
        if u in via_two:
            i = via_two.index(u)
            return remote(unit_src(u), relay_buf.at[i], unit_send.at[u], relay_recv.at[i], at(-1))
        if u in via_zero:
            i = via_zero.index(u)
            return remote(unit_src(u), relay_buf.at[i], unit_send.at[u], relay_recv.at[i], at(-3))
        return remote(unit_src(u), halo.at[u], unit_send.at[u], unit_recv.at[u], at(1))

    near_units = [u for u in range(units) if u % 4 < 2]

    def q_copy(h):
        return remote(
            q_hbm.at[pl.ds(0, tile), pl.ds(h * HEAD_DIM, HEAD_DIM)],
            q_next.at[h],
            q_send_sem.at[h],
            q_recv_sem.at[h],
            at(-1),
        )

    @pl.when(x == 3)
    def _():
        for u in range(units):
            far_copy(u).start()

    @pl.when(x < 3)
    def _():
        for u in near_units:
            near_copy(u).start()

    @pl.when(x > 0)
    def _():
        for h in range(heads):
            q_copy(h).start()

    def relay_copy(i, at_x):
        if at_x == 0:
            u = via_zero[i]
            return remote(relay_buf.at[i], halo.at[u], relay_send.at[i], unit_recv.at[u], at(4))
        if at_x == 1:
            u = via_two[i]
            return remote(relay_buf.at[i], halo.at[u], relay_send.at[i], unit_recv.at[u], at(-1))
        return remote(relay_buf.at[i], relay_buf.at[i], relay_send.at[i], relay_recv.at[i], at(3))

    def relay_count(at_x):
        return len(via_zero) if at_x == 0 else len(via_two)

    def relay(i, places):
        for at_x in places:
            if i < relay_count(at_x):

                @pl.when(x == at_x)
                def _(at_x=at_x):
                    copy = remote(relay_buf.at[i], relay_buf.at[i], relay_send.at[i], relay_recv.at[i], at(3))
                    copy.wait_recv()
                    relay_copy(i, at_x).start()

    for d in range(1, group):
        other = lax.rem(me + group - d, group)
        remote(stats.at[other], stats.at[other], stat_send.at[d], stat_recv.at[other], at(1)).wait_recv()
    inv_own[...] = lax.rsqrt(jnp.sum(stats[...], axis=0) / model + NORM_EPS)

    def inv_copy(side):
        dst = (inv_prev, inv_next)[side]
        return remote(inv_own, dst, inv_sem.at[side], inv_sem.at[2 + side], at((1, -1)[side]))

    inv_copy(0).start()

    @pl.when(x > 0)
    def _():
        inv_copy(1).start()

    def to_columns(row):
        return jnp.transpose(jnp.broadcast_to(row, (HEAD_DIM, row.shape[1])))

    def normed(values, column, gain):
        return (values.astype(F32) * column * gain).astype(BF16)

    def gain_row(ref, h):
        return ref[h]

    col_own[...] = to_columns(inv_own[...])

    def norm_own(h, carry):
        ql[h] = normed(ql[h], col_own[:rows], gain_row(qg_ref, h))
        kl[h] = normed(kl[h], col_own[rows:], gain_row(kg_ref, h))
        return carry

    lax.fori_loop(0, heads, norm_own, 0)
    for copy in loads(2):
        copy.wait()

    def seen(h, t, back):
        target = t - back
        count = count_ref[h, t]
        hit = jnp.int32(0)
        for w in range(WIN):
            hit = hit + jnp.where((tiles_ref[h, w, t] == target) & (w < count), 1, 0)
        return jnp.where((hit > 0) & (target >= 0), 1.0, 0.0).astype(F32)

    def top(scores, flag):
        return jnp.max(scores, axis=0, keepdims=True) * flag + (1.0 - flag) * LOW

    def shift(peak, flag):
        return peak * flag + (1.0 - flag) * HIGH

    def exps(scores, shifted):
        return jnp.exp2((scores - shifted) * EXP_SCALE)

    def row_sum(values):
        return jnp.sum(values, axis=0, keepdims=True)

    def two_blocks(keys, values, queries, flag_lo, flag_hi):
        scores = dot_nt(keys, queries)
        s_lo, s_hi = scores[:tile], scores[tile:]
        m_lo = top(s_lo, flag_lo)
        m_hi = jnp.max(s_hi, axis=0, keepdims=True) if flag_hi is None else top(s_hi, flag_hi)
        peak = jnp.maximum(m_lo, m_hi)
        p_lo = exps(s_lo, shift(peak, flag_lo))
        p_hi = exps(s_hi, peak if flag_hi is None else shift(peak, flag_hi))
        total = row_sum(p_lo) + row_sum(p_hi)
        mixed = dot_tn(values[:tile], p_lo.astype(BF16)) + dot_tn(values[tile:], p_hi.astype(BF16))
        return peak, total, mixed

    def local(h, carry):
        keys, values = kl[h], vl[h]
        scores = dot_nt(keys[:tile], ql[h, :tile])
        peak = jnp.max(scores, axis=0, keepdims=True)
        probs = exps(scores, peak)
        ml[h, 0:1] = peak
        ml[h, 1:2] = row_sum(probs)
        acc[h, 0] = dot_tn(values[:tile], probs.astype(BF16))
        peak, total, mixed = two_blocks(keys, values, ql[h, tile:], seen(h, first + 1, 1), None)
        ml[h, 2:3] = peak
        ml[h, 3:4] = total
        acc[h, 1] = mixed
        return carry

    def o_copy(h):
        return remote(o_send.at[h], o_recv.at[h], o_send_sem.at[h], o_recv_sem.at[h], at(1))

    def ml_copy():
        return remote(ml_send, ml_recv, ml_sem.at[0], ml_sem.at[1], at(1))

    def for_next(h, carry):
        q_copy(h).wait_recv()
        queries = normed(q_next[h], col_next[...], gain_row(qg_ref, h))
        peak, total, mixed = two_blocks(
            kl[h], vl[h], queries, seen(h, first + 2, 2), seen(h, first + 2, 1)
        )
        ml_send[h, 0:1] = peak
        ml_send[h, 1:2] = total
        o_send[h] = mixed.astype(BF16)
        o_copy(h).start()
        return carry

    relay(0, (0, 2))
    lax.fori_loop(0, heads, local, 0)
    relay(1, (0, 2))

    @pl.when(x < 3)
    def _():
        inv_copy(1).wait_recv()
        col_next[...] = to_columns(inv_next[:, :tile])
        lax.fori_loop(0, heads, for_next, 0)
        ml_copy().start()

    inv_copy(0).wait_recv()
    col_prev[...] = to_columns(inv_prev[:, rows:])

    def finish(h, part, total, mixed):
        out_buf[h, part * tile : (part + 1) * tile] = jnp.transpose(mixed * (1.0 / total)).astype(BF16)

    def out_copy(h):
        return pltpu.make_async_copy(
            out_buf.at[h], out_hbm.at[:, pl.ds(pl.multiple_of(h * HEAD_DIM, HEAD_DIM), HEAD_DIM)], out_sem.at[h]
        )

    def unit_wait(u):
        remote(halo.at[u], halo.at[u], unit_send.at[u], unit_recv.at[u], at(1)).wait_recv()

    def high_tile(h):
        keys = normed(halo[4 * h], col_prev[tile:], gain_row(kg_ref, h))
        values = halo[4 * h + 1]
        flag = seen(h, first + 1, 2)
        scores = dot_nt(keys, ql[h, tile:])
        before = ml[h, 2:3]
        peak = jnp.maximum(before, top(scores, flag))
        probs = exps(scores, shift(peak, flag))
        fade = exps(before, peak)
        total = ml[h, 3:4] * fade + row_sum(probs)
        mixed = acc[h, 1] * fade + dot_tn(values, probs.astype(BF16))
        finish(h, 1, total, mixed)
        return keys

    def far_head(h):
        for part in range(4):
            unit_wait(4 * h + part)
        keys_hi = high_tile(h)
        keys_lo = normed(halo[4 * h + 2], col_prev[:tile], gain_row(kg_ref, h))
        keys = jnp.concatenate([keys_lo, keys_hi], axis=0)
        values = jnp.concatenate([halo[4 * h + 3], halo[4 * h + 1]], axis=0)
        peak_far, total_far, mixed_far = two_blocks(
            keys, values, ql[h, :tile], seen(h, first, 2), seen(h, first, 1)
        )
        merge(h, peak_far, total_far, mixed_far)

    def merge(h, peak_far, total_far, mixed_far):
        before = ml[h, 0:1]
        peak = jnp.maximum(before, peak_far)
        fade, fade_far = exps(before, peak), exps(peak_far, peak)
        finish(h, 0, ml[h, 1:2] * fade + total_far * fade_far, acc[h, 0] * fade + mixed_far * fade_far)
        out_copy(h).start()

    def near_high(h, carry):
        unit_wait(4 * h)
        unit_wait(4 * h + 1)
        high_tile(h)
        return carry

    def near_low(h, carry):
        o_copy(h).wait_recv()
        merge(h, ml_recv[h, 0:1], ml_recv[h, 1:2], o_recv[h].astype(F32))
        return carry

    def loop(lo, hi, body):
        lax.fori_loop(lo, hi, lambda h, c: body(h, c), 0)

    @pl.when(x == 0)
    def _():
        done = 2
        for h in range(heads):
            need = (4 * h + 2) // 3 + 2
            while done < min(need, len(via_zero)):
                relay(done, (0,))
                done += 1
            far_head(h)
        while done < len(via_zero):
            relay(done, (0,))
            done += 1

    for at_x, start in ((1, 0), (2, 2)):

        @pl.when(x == at_x)
        def _(at_x=at_x, start=start):
            left = list(range(start, len(via_two)))
            split = max(0, len(left) - heads)
            for i in left[:split]:
                relay(i, (at_x,))
            left = left[split:]
            for h in range(heads):
                if h < len(left):
                    relay(left[h], (at_x,))
                near_high(h, 0)

    @pl.when(x == 3)
    def _():
        loop(0, heads, near_high)

    @pl.when(x > 0)
    def _():
        ml_copy().wait_recv()
        loop(0, heads, near_low)

    for h in range(heads):
        out_copy(h).wait()
    for d in range(1, group):
        stat_copy(d).wait_send()
    inv_copy(0).wait_send()

    @pl.when(x > 0)
    def _():
        inv_copy(1).wait_send()
        for h in range(heads):
            q_copy(h).wait_send()

    @pl.when(x == 3)
    def _():
        for u in range(units):
            far_copy(u).wait_send()

    @pl.when(x < 3)
    def _():
        for u in near_units:
            near_copy(u).wait_send()
        for h in range(heads):
            o_copy(h).wait_send()
        ml_copy().wait_send()

    for at_x in range(3):

        @pl.when(x == at_x)
        def _(at_x=at_x):
            for i in range(relay_count(at_x)):
                relay_copy(i, at_x).wait_send()


def per_device(q_proj, k_proj, v_proj, q_gain, k_gain, window_tiles, window_count):
    seqs, group = lax.axis_size("seq"), lax.axis_size("head")
    rows, cols = q_proj.shape
    heads, tile = cols // HEAD_DIM, rows // 2
    units = 4 * heads
    via_two, via_zero, _ = routes(heads)
    slots = max(len(via_two), len(via_zero))
    dma = pltpu.SemaphoreType.DMA
    anywhere = pl.BlockSpec(memory_space=pl.ANY)
    vmem = pl.BlockSpec(memory_space=pltpu.VMEM)
    smem = pl.BlockSpec(memory_space=pltpu.SMEM)
    flops = 30 * heads * tile * tile * HEAD_DIM
    return pl.pallas_call(
        functools.partial(kernel, seqs, group),
        out_shape=jax.ShapeDtypeStruct((rows, cols), BF16),
        in_specs=[anywhere] * 3 + [vmem] * 2 + [smem] * 2,
        out_specs=anywhere,
        scratch_shapes=[
            pltpu.VMEM((heads, rows, HEAD_DIM), BF16),
            pltpu.VMEM((heads, rows, HEAD_DIM), BF16),
            pltpu.VMEM((heads, rows, HEAD_DIM), BF16),
            pltpu.VMEM((units, tile, HEAD_DIM), BF16),
            pltpu.VMEM((slots, tile, HEAD_DIM), BF16),
            pltpu.VMEM((heads, tile, HEAD_DIM), BF16),
            pltpu.VMEM((heads, HEAD_DIM, tile), BF16),
            pltpu.VMEM((heads, HEAD_DIM, tile), BF16),
            pltpu.VMEM((heads, 2, tile), F32),
            pltpu.VMEM((heads, 2, tile), F32),
            pltpu.VMEM((heads, 2, HEAD_DIM, tile), F32),
            pltpu.VMEM((heads, 4, tile), F32),
            pltpu.VMEM((2 * rows, HEAD_DIM), F32),
            pltpu.VMEM((rows, HEAD_DIM), F32),
            pltpu.VMEM((tile, HEAD_DIM), F32),
            pltpu.VMEM((group, 1, 2 * rows), F32),
            pltpu.VMEM((1, 2 * rows), F32),
            pltpu.VMEM((1, 2 * rows), F32),
            pltpu.VMEM((1, 2 * rows), F32),
            pltpu.VMEM((heads, rows, HEAD_DIM), BF16),
            dma((3, heads)),
            dma((units,)),
            dma((units,)),
            dma((slots,)),
            dma((slots,)),
            dma((heads,)),
            dma((heads,)),
            dma((heads,)),
            dma((heads,)),
            dma((2,)),
            dma((group,)),
            dma((group,)),
            dma((4,)),
            dma((heads,)),
        ],
        compiler_params=pltpu.CompilerParams(
            collective_id=0, has_side_effects=True, vmem_limit_bytes=48 * 1024 * 1024
        ),
        cost_estimate=pl.CostEstimate(flops=flops, bytes_accessed=4 * rows * cols * 2, transcendentals=0),
        name="window_attention",
    )(
        q_proj,
        k_proj,
        v_proj,
        q_gain.reshape(heads, 1, HEAD_DIM),
        k_gain.reshape(heads, 1, HEAD_DIM),
        window_tiles.transpose(0, 2, 1),
        window_count,
    )


def solution(mesh):
    return jax.shard_map(
        per_device,
        mesh=mesh,
        in_specs=(
            P("seq", "head"),
            P("seq", "head"),
            P("seq", "head"),
            P("head"),
            P("head"),
            P("head", None, None),
            P("head", None),
        ),
        out_specs=P("seq", "head"),
        check_vma=False,
    )
```

```python
import functools
import math

import jax
import jax.numpy as jnp
from jax import lax
from jax.experimental import pallas as pl
from jax.experimental.pallas import tpu as pltpu
from jax.sharding import PartitionSpec as P

HEAD_DIM = 128
WIN = 3
NORM_EPS = 1e-06
EXP_SCALE = math.log2(math.e) / math.sqrt(HEAD_DIM)
LOW = -1e30
HIGH = 1e30
F32 = jnp.float32
BF16 = jnp.bfloat16
MESH = pl.DeviceIdType.MESH


def dot_nt(a, b):
    return lax.dot_general(a, b, (((1,), (1,)), ((), ())), preferred_element_type=F32)


def dot_tn(a, b):
    return lax.dot_general(a, b, (((0,), (0,)), ((), ())), preferred_element_type=F32)


SUB = 2
FAR_EARLY = 3
NEAR_EARLY = 2


def routes(heads):
    chunks = 4 * heads * SUB
    two, zero = (chunks * 3) // 10, (chunks * 13) // 40
    via_two = [3 * i for i in range(two)]
    via_zero = [3 * i + 1 for i in range(zero)]
    direct = [c for c in range(chunks) if c not in via_two and c not in via_zero]
    return via_two, via_zero, direct


def kernel(
    seqs,
    group,
    q_hbm,
    k_hbm,
    v_hbm,
    qg_ref,
    kg_ref,
    tiles_ref,
    count_ref,
    out_hbm,
    ql,
    kl,
    vl,
    qn,
    kn,
    halo,
    relay_buf,
    q_next,
    o_send,
    o_recv,
    ml_send,
    ml_recv,
    acc,
    ml,
    col_own,
    col_prev,
    col_next,
    stats,
    inv_own,
    inv_prev,
    inv_next,
    out_buf,
    load_sem,
    unit_send,
    unit_recv,
    relay_send,
    relay_recv,
    q_send_sem,
    q_recv_sem,
    o_send_sem,
    o_recv_sem,
    ml_sem,
    stat_send,
    stat_recv,
    inv_sem,
    out_sem,
):
    heads, rows, _ = ql.shape
    tile = rows // 2
    model = heads * HEAD_DIM * group
    piece = tile // SUB
    chunks = 4 * heads * SUB
    via_two, via_zero, direct = routes(heads)
    s = lax.axis_index("seq")
    me = lax.axis_index("head")
    x = lax.rem(s, 4)
    first = s * 2

    def at(step):
        return {"seq": lax.rem(s + step + seqs, seqs), "head": me}

    def remote(src, dst, send, recv, where):
        return pltpu.make_async_remote_copy(
            src_ref=src, dst_ref=dst, send_sem=send, recv_sem=recv, device_id=where, device_id_type=MESH
        )

    def loads(which):
        src, dst = ((q_hbm, ql), (k_hbm, kl), (v_hbm, vl))[which]
        return [
            pltpu.make_async_copy(src.at[:, pl.ds(h * HEAD_DIM, HEAD_DIM)], dst.at[h], load_sem.at[which, h])
            for h in range(heads)
        ]

    for which in range(3):
        for copy in loads(which):
            copy.start()

    barrier = pltpu.get_barrier_semaphore()

    def greet(where):
        pl.semaphore_signal(barrier, inc=1, device_id=where, device_id_type=MESH)

    greet(at(1))
    greet(at(-1))

    @pl.when((x == 0) | (x == 2))
    def _():
        greet(at(3))

    @pl.when((x == 1) | (x == 3))
    def _():
        greet(at(-3))

    @pl.when(x == 0)
    def _():
        greet(at(4))
        greet(at(-4))

    for d in range(1, group):
        greet({"seq": s, "head": lax.rem(me + d, group)})

    ones = jnp.ones((8, HEAD_DIM), BF16)
    for which, buf in ((0, ql), (1, kl)):
        for copy in loads(which):
            copy.wait()

        def square_sum(h, total, buf=buf):
            wide = buf[h].astype(F32)
            sq = wide * wide
            hi = sq.astype(BF16)
            lo = (sq - hi.astype(F32)).astype(BF16)
            return total + dot_nt(ones, hi) + dot_nt(ones, lo)

        total = lax.fori_loop(0, heads, square_sum, jnp.zeros((8, rows), F32))
        stats[me, :, which * rows : (which + 1) * rows] = total[:1]

    for copy in loads(2):
        copy.wait()

    @pl.when(x == 0)
    def _():
        pl.semaphore_wait(barrier, group - 1 + 5)

    @pl.when(x > 0)
    def _():
        pl.semaphore_wait(barrier, group - 1 + 3)

    def stat_copy(d):
        return remote(
            stats.at[me], stats.at[me], stat_send.at[d], stat_recv.at[me], {"seq": s, "head": lax.rem(me + d, group)}
        )

    for d in range(1, group):
        stat_copy(d).start()

    def chunk_src(c):
        h, part, sub = c // (4 * SUB), (c // SUB) % 4, c % SUB
        src = vl if part % 2 else kl
        return src.at[h, pl.ds((0 if part >= 2 else tile) + sub * piece, piece)]

    def near_copies(h):
        return [
            remote(
                src.at[h, pl.ds(tile + sub * piece, piece)],
                halo.at[4 * SUB * h + part * SUB + sub],
                unit_send.at[4 * SUB * h + part * SUB + sub],
                unit_recv.at[4 * SUB * h + part * SUB + sub],
                at(1),
            )
            for part, src in ((0, kl), (1, vl))
            for sub in range(SUB)
        ]

    def far_copy(c):
        if c in via_two:
            i = via_two.index(c)
            return remote(chunk_src(c), relay_buf.at[i], unit_send.at[c], relay_recv.at[i], at(-1))
        if c in via_zero:
            i = via_zero.index(c)
            return remote(chunk_src(c), relay_buf.at[i], unit_send.at[c], relay_recv.at[i], at(-3))
        return remote(chunk_src(c), halo.at[c], unit_send.at[c], unit_recv.at[c], at(1))

    def q_copy(h):
        return remote(ql.at[h, pl.ds(0, tile)], q_next.at[h], q_send_sem.at[h], q_recv_sem.at[h], at(-1))

    early = min(FAR_EARLY, chunks)
    near_early = min(NEAR_EARLY, heads)

    @pl.when(x == 3)
    def _():
        for c in range(early):
            far_copy(c).start()
            if c % 2 == 1 and c // 2 < heads:
                q_copy(c // 2).start()
        for h in range(early // 2, heads):
            q_copy(h).start()

    @pl.when((x > 0) & (x < 3))
    def _():
        for h in range(heads):
            q_copy(h).start()

    @pl.when(x < 3)
    def _():
        for h in range(near_early):
            for copy in near_copies(h):
                copy.start()

    def relay_copy(i, at_x):
        if at_x == 0:
            return remote(relay_buf.at[i], halo.at[3 * i + 1], relay_send.at[i], unit_recv.at[3 * i + 1], at(4))
        if at_x == 1:
            return remote(relay_buf.at[i], halo.at[3 * i], relay_send.at[i], unit_recv.at[3 * i], at(-1))
        return remote(relay_buf.at[i], relay_buf.at[i], relay_send.at[i], relay_recv.at[i], at(3))

    def relay_count(at_x):
        return len(via_zero) if at_x == 0 else len(via_two)

    def relay(i, places):
        for at_x in places:

            @pl.when((x == at_x) & (i < relay_count(at_x)))
            def _(at_x=at_x):
                remote(relay_buf.at[i], relay_buf.at[i], relay_send.at[i], relay_recv.at[i], at(3)).wait_recv()
                relay_copy(i, at_x).start()

    for d in range(1, group):
        other = lax.rem(me + group - d, group)
        remote(stats.at[other], stats.at[other], stat_send.at[d], stat_recv.at[other], at(1)).wait_recv()
    inv_own[...] = lax.rsqrt(jnp.sum(stats[...], axis=0) / model + NORM_EPS)

    def inv_copy(side):
        dst = (inv_prev, inv_next)[side]
        return remote(inv_own, dst, inv_sem.at[side], inv_sem.at[2 + side], at((1, -1)[side]))

    inv_copy(0).start()

    @pl.when(x > 0)
    def _():
        inv_copy(1).start()

    @pl.when(x == 3)
    def _():
        for c in range(early, chunks):
            far_copy(c).start()

    def to_columns(row):
        return jnp.transpose(jnp.broadcast_to(row, (HEAD_DIM, row.shape[1])))

    def normed(values, column, gain):
        return (values.astype(F32) * column * gain).astype(BF16)

    def gain_row(ref, h):
        return ref[pl.ds(pl.multiple_of(h * HEAD_DIM, HEAD_DIM), HEAD_DIM)].reshape(1, HEAD_DIM)

    col_own[...] = to_columns(inv_own[...])

    def norm_own(h, carry):
        qn[h] = normed(ql[h], col_own[:rows], gain_row(qg_ref, h))
        kn[h] = normed(kl[h], col_own[rows:], gain_row(kg_ref, h))
        return carry

    lax.fori_loop(0, heads, norm_own, 0)

    def seen(h, t, back):
        target = t - back
        count = count_ref[h, t]
        hit = jnp.int32(0)
        for w in range(WIN):
            hit = hit + jnp.where((tiles_ref[h, w, t] == target) & (w < count), 1, 0)
        return jnp.where((hit > 0) & (target >= 0), 1.0, 0.0).astype(F32)

    def top(scores, flag):
        return jnp.max(scores, axis=0, keepdims=True) * flag + (1.0 - flag) * LOW

    def shift(peak, flag):
        return peak * flag + (1.0 - flag) * HIGH

    def exps(scores, shifted):
        return jnp.exp2((scores - shifted) * EXP_SCALE)

    def row_sum(values):
        return jnp.sum(values, axis=0, keepdims=True)

    def two_blocks(keys, values, queries, flag_lo, flag_hi):
        scores = dot_nt(keys, queries)
        s_lo, s_hi = scores[:tile], scores[tile:]
        m_lo = top(s_lo, flag_lo)
        m_hi = jnp.max(s_hi, axis=0, keepdims=True) if flag_hi is None else top(s_hi, flag_hi)
        peak = jnp.maximum(m_lo, m_hi)
        p_lo = exps(s_lo, shift(peak, flag_lo))
        p_hi = exps(s_hi, peak if flag_hi is None else shift(peak, flag_hi))
        total = row_sum(p_lo) + row_sum(p_hi)
        mixed = dot_tn(values[:tile], p_lo.astype(BF16)) + dot_tn(values[tile:], p_hi.astype(BF16))
        return peak, total, mixed

    def local(h, carry):
        keys, values = kn[h], vl[h]
        scores = dot_nt(keys[:tile], qn[h, :tile])
        peak = jnp.max(scores, axis=0, keepdims=True)
        probs = exps(scores, peak)
        ml[h, 0:1] = peak
        ml[h, 1:2] = row_sum(probs)
        acc[h, 0] = dot_tn(values[:tile], probs.astype(BF16))
        peak, total, mixed = two_blocks(keys, values, qn[h, tile:], seen(h, first + 1, 1), None)
        ml[h, 2:3] = peak
        ml[h, 3:4] = total
        acc[h, 1] = mixed
        return carry

    def o_copy(h):
        return remote(o_send.at[h], o_recv.at[h], o_send_sem.at[h], o_recv_sem.at[h], at(1))

    def ml_copy():
        return remote(ml_send, ml_recv, ml_sem.at[0], ml_sem.at[1], at(1))

    def for_next(h, carry):
        q_copy(h).wait_recv()
        queries = normed(q_next[h], col_next[...], gain_row(qg_ref, h))
        peak, total, mixed = two_blocks(
            kn[h], vl[h], queries, seen(h, first + 2, 2), seen(h, first + 2, 1)
        )
        ml_send[h, 0:1] = peak
        ml_send[h, 1:2] = total
        o_send[h] = mixed.astype(BF16)
        o_copy(h).start()
        return carry

    def local_step(h, carry):
        relay(h, (0, 2))

        @pl.when((x < 3) & (h + near_early < heads))
        def _():
            for copy in near_copies(h + near_early):
                copy.start()

        return local(h, carry)

    lax.fori_loop(0, heads, local_step, 0)

    @pl.when(x < 3)
    def _():
        inv_copy(1).wait_recv()
        col_next[...] = to_columns(inv_next[:, :tile])

        def next_step(h, carry):
            relay(h, (1,))
            relay(heads + h, (0, 2))
            return for_next(h, carry)

        lax.fori_loop(0, heads, next_step, 0)
        ml_copy().start()

    inv_copy(0).wait_recv()
    col_prev[...] = to_columns(inv_prev[:, rows:])

    def finish(h, part, total, mixed):
        out_buf[h, part * tile : (part + 1) * tile] = jnp.transpose(mixed * (1.0 / total)).astype(BF16)

    def out_copy(h):
        return pltpu.make_async_copy(
            out_buf.at[h], out_hbm.at[:, pl.ds(pl.multiple_of(h * HEAD_DIM, HEAD_DIM), HEAD_DIM)], out_sem.at[h]
        )

    def part_wait(h, part):
        for sub in range(SUB):
            c = (4 * h + part) * SUB + sub
            remote(halo.at[c], halo.at[c], unit_send.at[c], unit_recv.at[c], at(1)).wait_recv()

    def arrived(h, part):
        return halo[pl.ds((4 * h + part) * SUB, SUB)].reshape(tile, HEAD_DIM)

    def high_tile(h):
        keys = normed(arrived(h, 0), col_prev[tile:], gain_row(kg_ref, h))
        values = arrived(h, 1)
        flag = seen(h, first + 1, 2)
        scores = dot_nt(keys, qn[h, tile:])
        before = ml[h, 2:3]
        peak = jnp.maximum(before, top(scores, flag))
        probs = exps(scores, shift(peak, flag))
        fade = exps(before, peak)
        total = ml[h, 3:4] * fade + row_sum(probs)
        mixed = acc[h, 1] * fade + dot_tn(values, probs.astype(BF16))
        finish(h, 1, total, mixed)
        return keys

    def far_head(h):
        for part in range(4):
            part_wait(h, part)
        keys_hi = high_tile(h)
        keys_lo = normed(arrived(h, 2), col_prev[:tile], gain_row(kg_ref, h))
        keys = jnp.concatenate([keys_lo, keys_hi], axis=0)
        values = jnp.concatenate([arrived(h, 3), arrived(h, 1)], axis=0)
        peak_far, total_far, mixed_far = two_blocks(
            keys, values, qn[h, :tile], seen(h, first, 2), seen(h, first, 1)
        )
        merge(h, peak_far, total_far, mixed_far)

    def merge(h, peak_far, total_far, mixed_far):
        before = ml[h, 0:1]
        peak = jnp.maximum(before, peak_far)
        fade, fade_far = exps(before, peak), exps(peak_far, peak)
        finish(h, 0, ml[h, 1:2] * fade + total_far * fade_far, acc[h, 0] * fade + mixed_far * fade_far)
        out_copy(h).start()

    def near_high(h, carry):
        part_wait(h, 0)
        part_wait(h, 1)
        high_tile(h)
        return carry

    def near_low(h, carry):
        o_copy(h).wait_recv()
        merge(h, ml_recv[h, 0:1], ml_recv[h, 1:2], o_recv[h].astype(F32))
        return carry

    def loop(lo, hi, body):
        lax.fori_loop(lo, hi, lambda h, c: body(h, c), 0)

    def relays(lo, hi, at_x):
        loop(lo, hi, lambda i, c: (relay(i, (at_x,)), c)[1])

    @pl.when(x == 0)
    def _():
        relays(2 * heads, len(via_zero), 0)
        loop(0, heads, lambda h, c: (far_head(h), c)[1])

    @pl.when(x == 1)
    def _():
        def step(h, carry):
            relay(heads + h, (1,))
            return near_high(h, carry)

        loop(0, heads, step)
        relays(2 * heads, len(via_two), 1)

    @pl.when(x == 2)
    def _():
        relays(2 * heads, len(via_two), 2)
        loop(0, heads, near_high)

    @pl.when(x == 3)
    def _():
        loop(0, heads, near_high)

    @pl.when(x > 0)
    def _():
        ml_copy().wait_recv()
        loop(0, heads, near_low)

    for h in range(heads):
        out_copy(h).wait()
    for d in range(1, group):
        stat_copy(d).wait_send()
    inv_copy(0).wait_send()

    @pl.when(x > 0)
    def _():
        inv_copy(1).wait_send()
        for h in range(heads):
            q_copy(h).wait_send()

    @pl.when(x == 3)
    def _():
        for c in range(chunks):
            far_copy(c).wait_send()

    @pl.when(x < 3)
    def _():
        for h in range(heads):
            for copy in near_copies(h):
                copy.wait_send()
            o_copy(h).wait_send()
        ml_copy().wait_send()

    for at_x in range(3):

        @pl.when(x == at_x)
        def _(at_x=at_x):
            for i in range(relay_count(at_x)):
                relay_copy(i, at_x).wait_send()


def per_device(q_proj, k_proj, v_proj, q_gain, k_gain, window_tiles, window_count):
    seqs, group = lax.axis_size("seq"), lax.axis_size("head")
    rows, cols = q_proj.shape
    heads, tile = cols // HEAD_DIM, rows // 2
    chunks = 4 * heads * SUB
    via_two, via_zero, _ = routes(heads)
    slots = max(len(via_two), len(via_zero))
    dma = pltpu.SemaphoreType.DMA
    anywhere = pl.BlockSpec(memory_space=pl.ANY)
    vmem = pl.BlockSpec(memory_space=pltpu.VMEM)
    smem = pl.BlockSpec(memory_space=pltpu.SMEM)
    flops = 30 * heads * tile * tile * HEAD_DIM
    return pl.pallas_call(
        functools.partial(kernel, seqs, group),
        out_shape=jax.ShapeDtypeStruct((rows, cols), BF16),
        in_specs=[anywhere] * 3 + [vmem] * 2 + [smem] * 2,
        out_specs=anywhere,
        scratch_shapes=[
            pltpu.VMEM((heads, rows, HEAD_DIM), BF16),
            pltpu.VMEM((heads, rows, HEAD_DIM), BF16),
            pltpu.VMEM((heads, rows, HEAD_DIM), BF16),
            pltpu.VMEM((heads, rows, HEAD_DIM), BF16),
            pltpu.VMEM((heads, rows, HEAD_DIM), BF16),
            pltpu.VMEM((chunks, tile // SUB, HEAD_DIM), BF16),
            pltpu.VMEM((slots, tile // SUB, HEAD_DIM), BF16),
            pltpu.VMEM((heads, tile, HEAD_DIM), BF16),
            pltpu.VMEM((heads, HEAD_DIM, tile), BF16),
            pltpu.VMEM((heads, HEAD_DIM, tile), BF16),
            pltpu.VMEM((heads, 2, tile), F32),
            pltpu.VMEM((heads, 2, tile), F32),
            pltpu.VMEM((heads, 2, HEAD_DIM, tile), F32),
            pltpu.VMEM((heads, 4, tile), F32),
            pltpu.VMEM((2 * rows, HEAD_DIM), F32),
            pltpu.VMEM((rows, HEAD_DIM), F32),
            pltpu.VMEM((tile, HEAD_DIM), F32),
            pltpu.VMEM((group, 1, 2 * rows), F32),
            pltpu.VMEM((1, 2 * rows), F32),
            pltpu.VMEM((1, 2 * rows), F32),
            pltpu.VMEM((1, 2 * rows), F32),
            pltpu.VMEM((heads, rows, HEAD_DIM), BF16),
            dma((3, heads)),
            dma((chunks,)),
            dma((chunks,)),
            dma((slots,)),
            dma((slots,)),
            dma((heads,)),
            dma((heads,)),
            dma((heads,)),
            dma((heads,)),
            dma((2,)),
            dma((group,)),
            dma((group,)),
            dma((4,)),
            dma((heads,)),
        ],
        compiler_params=pltpu.CompilerParams(
            collective_id=0, has_side_effects=True, vmem_limit_bytes=62 * 1024 * 1024
        ),
        cost_estimate=pl.CostEstimate(flops=flops, bytes_accessed=4 * rows * cols * 2, transcendentals=0),
        name="window_attention",
    )(
        q_proj,
        k_proj,
        v_proj,
        q_gain,
        k_gain,
        window_tiles.transpose(0, 2, 1),
        window_count,
    )


def solution(mesh):
    return jax.shard_map(
        per_device,
        mesh=mesh,
        in_specs=(
            P("seq", "head"),
            P("seq", "head"),
            P("seq", "head"),
            P("head"),
            P("head"),
            P("head", None, None),
            P("head", None),
        ),
        out_specs=P("seq", "head"),
        check_vma=False,
    )
```

```python
import functools
import math

import jax
import jax.numpy as jnp
from jax import lax
from jax.experimental import pallas as pl
from jax.experimental.pallas import tpu as pltpu
from jax.sharding import PartitionSpec as P

HEAD_DIM = 128
WIN = 3
NORM_EPS = 1e-06
EXP_SCALE = math.log2(math.e) / math.sqrt(HEAD_DIM)
LOW = -1e30
HIGH = 1e30
F32 = jnp.float32
BF16 = jnp.bfloat16
MESH = pl.DeviceIdType.MESH


def dot_nt(a, b):
    return lax.dot_general(a, b, (((1,), (1,)), ((), ())), preferred_element_type=F32)


def dot_tn(a, b):
    return lax.dot_general(a, b, (((0,), (0,)), ((), ())), preferred_element_type=F32)


SUB = 2
FAR_EARLY = 3
FAR_AHEAD = 1
PER_DIRECT = 8
Q_EVERY = 7
NEAR_EARLY = 2


def two_slot(i):
    return 10 * (i // 2) + 6 * (i % 2)


def one_slot(i):
    return two_slot(i) + 1


def zero_slot(i):
    return 10 * (i // 3) + 3 * (i % 3) + 2


def routes(heads):
    chunks = 4 * heads * SUB
    via_two, via_one, via_zero = (
        [slot(i) for i in range(chunks) if slot(i) < chunks] for slot in (two_slot, one_slot, zero_slot)
    )
    direct = [c for c in range(chunks) if c not in via_two + via_one + via_zero]
    return via_two, via_one, via_zero, direct


def kernel(
    seqs,
    group,
    q_hbm,
    k_hbm,
    v_hbm,
    qg_in,
    kg_in,
    tiles_in,
    count_in,
    out_hbm,
    qg_ref,
    kg_ref,
    tiles_ref,
    count_ref,
    ql,
    kl,
    vl,
    qn,
    kn,
    halo,
    relay_buf,
    relay_b,
    q_next,
    o_send,
    o_recv,
    ml_send,
    ml_recv,
    acc,
    ml,
    col_own,
    col_prev,
    col_next,
    stats,
    inv_own,
    inv_prev,
    inv_next,
    out_buf,
    load_sem,
    small_sem,
    unit_send,
    unit_recv,
    relay_send,
    relay_recv,
    relay_b_send,
    relay_b_recv,
    q_send_sem,
    q_recv_sem,
    o_send_sem,
    o_recv_sem,
    ml_sem,
    stat_send,
    stat_recv,
    inv_sem,
    out_sem,
):
    heads, rows, _ = ql.shape
    tile = rows // 2
    model = heads * HEAD_DIM * group
    piece = tile // SUB
    chunks = 4 * heads * SUB
    via_two, via_one, via_zero, direct = routes(heads)
    s = lax.axis_index("seq")
    me = lax.axis_index("head")
    x = lax.rem(s, 4)
    first = s * 2

    def at(step):
        return {"seq": lax.rem(s + step + seqs, seqs), "head": me}

    def remote(src, dst, send, recv, where):
        return pltpu.make_async_remote_copy(
            src_ref=src, dst_ref=dst, send_sem=send, recv_sem=recv, device_id=where, device_id_type=MESH
        )

    barrier = pltpu.get_barrier_semaphore()

    def greet(where):
        pl.semaphore_signal(barrier, inc=1, device_id=where, device_id_type=MESH)

    greet(at(1))
    greet(at(-1))

    @pl.when((x == 0) | (x == 2))
    def _():
        greet(at(3))

    @pl.when((x == 1) | (x == 3))
    def _():
        greet(at(-3))

    @pl.when(x == 0)
    def _():
        greet(at(4))
        greet(at(-4))
        greet(at(-3))

    @pl.when(x == 1)
    def _():
        greet(at(3))

    for d in range(1, group):
        greet({"seq": s, "head": lax.rem(me + d, group)})

    def loads(which):
        src, dst = ((q_hbm, ql), (k_hbm, kl), (v_hbm, vl))[which]
        return [
            pltpu.make_async_copy(src.at[:, pl.ds(h * HEAD_DIM, HEAD_DIM)], dst.at[h], load_sem.at[which, h])
            for h in range(heads)
        ]

    small = [
        pltpu.make_async_copy(src, dst, small_sem.at[n])
        for n, (src, dst) in enumerate(
            ((qg_in, qg_ref), (kg_in, kg_ref), (tiles_in, tiles_ref), (count_in, count_ref))
        )
    ]
    for which in range(3):
        for copy in loads(which):
            copy.start()
    for copy in small:
        copy.start()

    ones = jnp.ones((8, HEAD_DIM), BF16)
    for which, buf in ((0, ql), (1, kl)):
        for copy in loads(which):
            copy.wait()

        def square_sum(h, total, buf=buf):
            wide = buf[h].astype(F32)
            return total + wide * wide

        left = lax.fori_loop(1, heads, square_sum, square_sum(0, 0.0))
        total = jnp.zeros((8, rows), F32)
        for _ in range(3):
            term = left.astype(BF16)
            total = total + dot_nt(ones, term)
            left = left - term.astype(F32)
        stats[me, :, which * rows : (which + 1) * rows] = total[:1]

    for copy in loads(2) + small:
        copy.wait()

    @pl.when(x == 0)
    def _():
        pl.semaphore_wait(barrier, group - 1 + 6)

    @pl.when(x == 1)
    def _():
        pl.semaphore_wait(barrier, group - 1 + 4)

    @pl.when(x > 1)
    def _():
        pl.semaphore_wait(barrier, group - 1 + 3)

    def stat_copy(d):
        return remote(
            stats.at[me], stats.at[me], stat_send.at[d], stat_recv.at[me], {"seq": s, "head": lax.rem(me + d, group)}
        )

    for d in range(1, group):
        stat_copy(d).start()

    def chunk_src(c):
        h, part, sub = c // (4 * SUB), (c // SUB) % 4, c % SUB
        src = vl if part % 2 else kl
        return src.at[h, pl.ds((0 if part >= 2 else tile) + sub * piece, piece)]

    def near_copies(h):
        return [
            remote(
                src.at[h, pl.ds(tile + sub * piece, piece)],
                halo.at[4 * SUB * h + part * SUB + sub],
                unit_send.at[4 * SUB * h + part * SUB + sub],
                unit_recv.at[4 * SUB * h + part * SUB + sub],
                at(1),
            )
            for part, src in ((0, kl), (1, vl))
            for sub in range(SUB)
        ]

    def far_copy(c):
        if c in via_two:
            i = via_two.index(c)
            return remote(chunk_src(c), relay_buf.at[i], unit_send.at[c], relay_recv.at[i], at(-1))
        if c in via_one:
            i = via_one.index(c)
            return remote(chunk_src(c), relay_b.at[i], unit_send.at[c], relay_b_recv.at[i], at(-1))
        if c in via_zero:
            i = via_zero.index(c)
            return remote(chunk_src(c), relay_buf.at[i], unit_send.at[c], relay_recv.at[i], at(-3))
        return remote(chunk_src(c), halo.at[c], unit_send.at[c], unit_recv.at[c], at(1))

    def q_copy(h):
        return remote(ql.at[h, pl.ds(0, tile)], q_next.at[h], q_send_sem.at[h], q_recv_sem.at[h], at(-1))

    early = sorted(via_one[:FAR_EARLY] + via_two[:FAR_EARLY] + via_zero[:FAR_EARLY])
    relayed = [c for c in sorted(via_one + via_two + via_zero) if c not in early]
    late, waiting = [], list(direct)
    while relayed or waiting:
        late, waiting = late + waiting[:1], waiting[1:]
        late, relayed = late + relayed[:PER_DIRECT], relayed[PER_DIRECT:]
    near_early = min(NEAR_EARLY, heads)

    @pl.when(x == 3)
    def _():
        for c in early:
            far_copy(c).start()
        q_copy(0).start()

    def near_start(h):
        for half in range(2):

            @pl.when(x < 3)
            def _(half=half):
                for copy in near_copies(h)[half * SUB : (half + 1) * SUB]:
                    copy.start()

            if half == 0:

                @pl.when((x > 0) & (x < 3))
                def _():
                    q_copy(h).start()

    for h in range(near_early):
        near_start(h)

    def relay_copy(i, at_x):
        if at_x == 0:
            return remote(relay_buf.at[i], halo.at[zero_slot(i)], relay_send.at[i], unit_recv.at[zero_slot(i)], at(4))
        if at_x == 1:
            return remote(relay_buf.at[i], halo.at[two_slot(i)], relay_send.at[i], unit_recv.at[two_slot(i)], at(-1))
        return remote(relay_buf.at[i], relay_buf.at[i], relay_send.at[i], relay_recv.at[i], at(3))

    def relay_count(at_x):
        return len(via_zero) if at_x == 0 else len(via_two)

    def relay(i, places):
        for at_x in places:

            @pl.when((x == at_x) & (i < relay_count(at_x)))
            def _(at_x=at_x):
                remote(relay_buf.at[i], relay_buf.at[i], relay_send.at[i], relay_recv.at[i], at(3)).wait_recv()
                relay_copy(i, at_x).start()

    def relay_b_copy(i, at_x):
        if at_x == 1:
            c = one_slot(i)
            return remote(relay_b.at[i], halo.at[c], relay_b_send.at[i], unit_recv.at[c], at(3))
        return remote(relay_b.at[i], relay_b.at[i], relay_b_send.at[i], relay_b_recv.at[i], at(-1))

    def relay_one(i, at_x):
        @pl.when((x == at_x) & (i < len(via_one)))
        def _():
            remote(relay_b.at[i], relay_b.at[i], relay_b_send.at[i], relay_b_recv.at[i], at(-1)).wait_recv()
            relay_b_copy(i, at_x).start()

    for d in range(1, group):
        other = lax.rem(me + group - d, group)
        remote(stats.at[other], stats.at[other], stat_send.at[d], stat_recv.at[other], at(1)).wait_recv()
    inv_own[...] = lax.rsqrt(jnp.sum(stats[...], axis=0) / model + NORM_EPS)

    def inv_copy(side):
        dst = (inv_prev, inv_next)[side]
        return remote(inv_own, dst, inv_sem.at[side], inv_sem.at[2 + side], at((1, -1)[side]))

    inv_copy(0).start()

    @pl.when(x > 0)
    def _():
        inv_copy(1).start()

    @pl.when(x == 3)
    def _():
        for n, c in enumerate(late):
            far_copy(c).start()
            if n % Q_EVERY == 1 and n // Q_EVERY + 1 < heads:
                q_copy(n // Q_EVERY + 1).start()
        for h in range((len(late) - 2) // Q_EVERY + 2, heads):
            q_copy(h).start()

    def to_columns(row):
        return jnp.transpose(jnp.broadcast_to(row, (HEAD_DIM, row.shape[1])))

    def normed(values, column, gain):
        return (values.astype(F32) * column * gain).astype(BF16)

    def gain_row(ref, h):
        return ref[pl.ds(pl.multiple_of(h * HEAD_DIM, HEAD_DIM), HEAD_DIM)].reshape(1, HEAD_DIM)

    col_own[...] = to_columns(inv_own[...])

    def norm_own(h, carry):
        qn[h] = normed(ql[h], col_own[:rows], gain_row(qg_ref, h))
        kn[h] = normed(kl[h], col_own[rows:], gain_row(kg_ref, h))
        return carry

    lax.fori_loop(0, heads, norm_own, 0)

    def seen(h, t, back):
        target = t - back
        count = count_ref[h, t]
        hit = jnp.int32(0)
        for w in range(WIN):
            hit = hit + jnp.where((tiles_ref[h, w, t] == target) & (w < count), 1, 0)
        return jnp.where((hit > 0) & (target >= 0), 1.0, 0.0).astype(F32)

    def top(scores, flag):
        return jnp.max(scores, axis=0, keepdims=True) * flag + (1.0 - flag) * LOW

    def shift(peak, flag):
        return peak * flag + (1.0 - flag) * HIGH

    def exps(scores, shifted):
        return jnp.exp2((scores - shifted) * EXP_SCALE)

    def row_sum(values):
        return jnp.sum(values, axis=0, keepdims=True)

    def two_blocks(keys, values, queries, flag_lo, flag_hi):
        scores = dot_nt(keys, queries)
        s_lo, s_hi = scores[:tile], scores[tile:]
        m_lo = top(s_lo, flag_lo)
        m_hi = jnp.max(s_hi, axis=0, keepdims=True) if flag_hi is None else top(s_hi, flag_hi)
        peak = jnp.maximum(m_lo, m_hi)
        p_lo = exps(s_lo, shift(peak, flag_lo))
        p_hi = exps(s_hi, peak if flag_hi is None else shift(peak, flag_hi))
        total = row_sum(p_lo) + row_sum(p_hi)
        mixed = dot_tn(values[:tile], p_lo.astype(BF16)) + dot_tn(values[tile:], p_hi.astype(BF16))
        return peak, total, mixed

    def local(h, carry):
        keys, values = kn[h], vl[h]
        scores = dot_nt(keys[:tile], qn[h, :tile])
        peak = jnp.max(scores, axis=0, keepdims=True)
        probs = exps(scores, peak)
        ml[h, 0:1] = peak
        ml[h, 1:2] = row_sum(probs)
        acc[h, 0] = dot_tn(values[:tile], probs.astype(BF16))
        peak, total, mixed = two_blocks(keys, values, qn[h, tile:], seen(h, first + 1, 1), None)
        ml[h, 2:3] = peak
        ml[h, 3:4] = total
        acc[h, 1] = mixed
        return carry

    def o_copy(h):
        return remote(o_send.at[h], o_recv.at[h], o_send_sem.at[h], o_recv_sem.at[h], at(1))

    def ml_copy():
        return remote(ml_send, ml_recv, ml_sem.at[0], ml_sem.at[1], at(1))

    def for_next(h, carry):
        q_copy(h).wait_recv()
        queries = normed(q_next[h], col_next[...], gain_row(qg_ref, h))
        peak, total, mixed = two_blocks(
            kn[h], vl[h], queries, seen(h, first + 2, 2), seen(h, first + 2, 1)
        )
        ml_send[h, 0:1] = peak
        ml_send[h, 1:2] = total
        o_send[h] = mixed.astype(BF16)
        o_copy(h).start()
        return carry

    def local_step(h, carry):
        relay_one(h, 2)
        relay(h, (0, 2))

        @pl.when(h + near_early < heads)
        def _():
            near_start(h + near_early)

        return local(h, carry)

    lax.fori_loop(0, heads, local_step, 0)

    @pl.when(x < 3)
    def _():
        inv_copy(1).wait_recv()
        col_next[...] = to_columns(inv_next[:, :tile])

        def next_step(h, carry):
            relay_one(heads + h, 2)
            relay(heads + h, (0, 2))
            relay_one(h, 1)
            relay(h, (1,))
            return for_next(h, carry)

        lax.fori_loop(0, heads, next_step, 0)
        ml_copy().start()

    inv_copy(0).wait_recv()
    col_prev[...] = to_columns(inv_prev[:, rows:])

    def finish(h, part, total, mixed):
        out_buf[h, part * tile : (part + 1) * tile] = jnp.transpose(mixed * (1.0 / total)).astype(BF16)

    def out_copy(h):
        return pltpu.make_async_copy(
            out_buf.at[h], out_hbm.at[:, pl.ds(pl.multiple_of(h * HEAD_DIM, HEAD_DIM), HEAD_DIM)], out_sem.at[h]
        )

    def part_wait(h, part):
        for sub in range(SUB):
            c = (4 * h + part) * SUB + sub
            remote(halo.at[c], halo.at[c], unit_send.at[c], unit_recv.at[c], at(1)).wait_recv()

    def arrived(h, part):
        return halo[pl.ds((4 * h + part) * SUB, SUB)].reshape(tile, HEAD_DIM)

    def high_tile(h):
        keys = normed(arrived(h, 0), col_prev[tile:], gain_row(kg_ref, h))
        values = arrived(h, 1)
        flag = seen(h, first + 1, 2)
        scores = dot_nt(keys, qn[h, tile:])
        before = ml[h, 2:3]
        peak = jnp.maximum(before, top(scores, flag))
        probs = exps(scores, shift(peak, flag))
        fade = exps(before, peak)
        total = ml[h, 3:4] * fade + row_sum(probs)
        mixed = acc[h, 1] * fade + dot_tn(values, probs.astype(BF16))
        finish(h, 1, total, mixed)
        return keys

    def far_head(h):
        for part in range(4):
            part_wait(h, part)
        keys_hi = high_tile(h)
        keys_lo = normed(arrived(h, 2), col_prev[:tile], gain_row(kg_ref, h))
        keys = jnp.concatenate([keys_lo, keys_hi], axis=0)
        values = jnp.concatenate([arrived(h, 3), arrived(h, 1)], axis=0)
        peak_far, total_far, mixed_far = two_blocks(
            keys, values, qn[h, :tile], seen(h, first, 2), seen(h, first, 1)
        )
        merge(h, peak_far, total_far, mixed_far)

    def merge(h, peak_far, total_far, mixed_far):
        before = ml[h, 0:1]
        peak = jnp.maximum(before, peak_far)
        fade, fade_far = exps(before, peak), exps(peak_far, peak)
        finish(h, 0, ml[h, 1:2] * fade + total_far * fade_far, acc[h, 0] * fade + mixed_far * fade_far)
        out_copy(h).start()

    def near_high(h, carry):
        part_wait(h, 0)
        part_wait(h, 1)
        high_tile(h)
        return carry

    def near_low(h, carry):
        o_copy(h).wait_recv()
        merge(h, ml_recv[h, 0:1], ml_recv[h, 1:2], o_recv[h].astype(F32))
        return carry

    def loop(lo, hi, body):
        lax.fori_loop(lo, hi, lambda h, c: body(h, c), 0)

    def relays(lo, hi, at_x):
        loop(lo, hi, lambda i, c: (relay(i, (at_x,)), c)[1])

    @pl.when(x == 0)
    def _():
        tail = len(via_zero) - 2 * heads

        relays(2 * heads, 2 * heads + tail - FAR_AHEAD, 0)

        def step(h, carry):
            relay(2 * heads + tail - FAR_AHEAD + h, (0,))
            far_head(h)
            return carry

        loop(0, heads, step)

    @pl.when(x == 1)
    def _():
        def step(h, carry):
            relay_one(heads + h, 1)
            relay(heads + h, (1,))
            return near_high(h, carry)

        loop(0, heads, step)
        relays(2 * heads, len(via_two), 1)

    @pl.when(x == 2)
    def _():
        relays(2 * heads, len(via_two), 2)
        loop(0, heads, near_high)

    @pl.when(x == 3)
    def _():
        loop(0, heads, near_high)

    @pl.when(x > 0)
    def _():
        ml_copy().wait_recv()
        loop(0, heads, near_low)

    for h in range(heads):
        out_copy(h).wait()
    for d in range(1, group):
        stat_copy(d).wait_send()
    inv_copy(0).wait_send()

    @pl.when(x > 0)
    def _():
        inv_copy(1).wait_send()
        for h in range(heads):
            q_copy(h).wait_send()

    @pl.when(x == 3)
    def _():
        for c in range(chunks):
            far_copy(c).wait_send()

    @pl.when(x < 3)
    def _():
        for h in range(heads):
            for copy in near_copies(h):
                copy.wait_send()
            o_copy(h).wait_send()
        ml_copy().wait_send()

    for at_x in range(3):

        @pl.when(x == at_x)
        def _(at_x=at_x):
            for i in range(relay_count(at_x)):
                relay_copy(i, at_x).wait_send()
            if at_x > 0:
                for i in range(len(via_one)):
                    relay_b_copy(i, at_x).wait_send()


def per_device(q_proj, k_proj, v_proj, q_gain, k_gain, window_tiles, window_count):
    seqs, group = lax.axis_size("seq"), lax.axis_size("head")
    rows, cols = q_proj.shape
    heads, tile = cols // HEAD_DIM, rows // 2
    chunks = 4 * heads * SUB
    via_two, via_one, via_zero, _ = routes(heads)
    slots = max(len(via_two), len(via_zero))
    slots_b = len(via_one)
    dma = pltpu.SemaphoreType.DMA
    anywhere = pl.BlockSpec(memory_space=pl.ANY)
    hbm = pl.BlockSpec(memory_space=pltpu.HBM)
    flops = 30 * heads * tile * tile * HEAD_DIM
    return pl.pallas_call(
        functools.partial(kernel, seqs, group),
        out_shape=jax.ShapeDtypeStruct((rows, cols), BF16),
        in_specs=[hbm] * 7,
        out_specs=anywhere,
        scratch_shapes=[
            pltpu.VMEM(q_gain.shape, F32),
            pltpu.VMEM(k_gain.shape, F32),
            pltpu.SMEM((heads, WIN, window_count.shape[1]), jnp.int32),
            pltpu.SMEM(window_count.shape, jnp.int32),
            pltpu.VMEM((heads, rows, HEAD_DIM), BF16),
            pltpu.VMEM((heads, rows, HEAD_DIM), BF16),
            pltpu.VMEM((heads, rows, HEAD_DIM), BF16),
            pltpu.VMEM((heads, rows, HEAD_DIM), BF16),
            pltpu.VMEM((heads, rows, HEAD_DIM), BF16),
            pltpu.VMEM((chunks, tile // SUB, HEAD_DIM), BF16),
            pltpu.VMEM((slots, tile // SUB, HEAD_DIM), BF16),
            pltpu.VMEM((slots_b, tile // SUB, HEAD_DIM), BF16),
            pltpu.VMEM((heads, tile, HEAD_DIM), BF16),
            pltpu.VMEM((heads, HEAD_DIM, tile), BF16),
            pltpu.VMEM((heads, HEAD_DIM, tile), BF16),
            pltpu.VMEM((heads, 2, tile), F32),
            pltpu.VMEM((heads, 2, tile), F32),
            pltpu.VMEM((heads, 2, HEAD_DIM, tile), F32),
            pltpu.VMEM((heads, 4, tile), F32),
            pltpu.VMEM((2 * rows, HEAD_DIM), F32),
            pltpu.VMEM((rows, HEAD_DIM), F32),
            pltpu.VMEM((tile, HEAD_DIM), F32),
            pltpu.VMEM((group, 1, 2 * rows), F32),
            pltpu.VMEM((1, 2 * rows), F32),
            pltpu.VMEM((1, 2 * rows), F32),
            pltpu.VMEM((1, 2 * rows), F32),
            pltpu.VMEM((heads, rows, HEAD_DIM), BF16),
            dma((3, heads)),
            dma((4,)),
            dma((chunks,)),
            dma((chunks,)),
            dma((slots,)),
            dma((slots,)),
            dma((slots_b,)),
            dma((slots_b,)),
            dma((heads,)),
            dma((heads,)),
            dma((heads,)),
            dma((heads,)),
            dma((2,)),
            dma((group,)),
            dma((group,)),
            dma((4,)),
            dma((heads,)),
        ],
        compiler_params=pltpu.CompilerParams(
            collective_id=0, has_side_effects=True, vmem_limit_bytes=62 * 1024 * 1024
        ),
        cost_estimate=pl.CostEstimate(flops=flops, bytes_accessed=4 * rows * cols * 2, transcendentals=0),
        name="window_attention",
    )(
        q_proj,
        k_proj,
        v_proj,
        q_gain,
        k_gain,
        window_tiles.transpose(0, 2, 1),
        window_count,
    )


def solution(mesh):
    return jax.shard_map(
        per_device,
        mesh=mesh,
        in_specs=(
            P("seq", "head"),
            P("seq", "head"),
            P("seq", "head"),
            P("head"),
            P("head"),
            P("head", None, None),
            P("head", None),
        ),
        out_specs=P("seq", "head"),
        check_vma=False,
    )
```

```python
import functools
import math

import jax
import jax.numpy as jnp
from jax import lax
from jax.experimental import pallas as pl
from jax.experimental.pallas import tpu as pltpu
from jax.sharding import PartitionSpec as P

HEAD_DIM = 128
WIN = 3
NORM_EPS = 1e-06
EXP_SCALE = math.log2(math.e) / math.sqrt(HEAD_DIM)
LOW = -1e30
HIGH = 1e30
F32 = jnp.float32
BF16 = jnp.bfloat16
MESH = pl.DeviceIdType.MESH


def dot_nt(a, b):
    return lax.dot_general(a, b, (((1,), (1,)), ((), ())), preferred_element_type=F32)


def dot_tn(a, b):
    return lax.dot_general(a, b, (((0,), (0,)), ((), ())), preferred_element_type=F32)


SUB = 2
FAR_EARLY = 3
FAR_AHEAD = 1
PER_DIRECT = 8
Q_EVERY = 7
NEAR_EARLY = 2


def two_slot(i):
    return 10 * (i // 2) + 6 * (i % 2)


def one_slot(i):
    return two_slot(i) + 1


def zero_slot(i):
    return 10 * (i // 3) + 3 * (i % 3) + 2


def routes(heads):
    chunks = 4 * heads * SUB
    via_two, via_one, via_zero = (
        [slot(i) for i in range(chunks) if slot(i) < chunks] for slot in (two_slot, one_slot, zero_slot)
    )
    direct = [c for c in range(chunks) if c not in via_two + via_one + via_zero]
    return via_two, via_one, via_zero, direct


def kernel(
    seqs,
    group,
    q_hbm,
    k_hbm,
    v_hbm,
    qg_in,
    kg_in,
    tiles_in,
    count_in,
    out_hbm,
    qg_ref,
    kg_ref,
    tiles_ref,
    count_ref,
    ql,
    kl,
    vl,
    qn,
    kn,
    halo,
    relay_buf,
    relay_b,
    q_next,
    o_send,
    o_recv,
    ml_send,
    ml_recv,
    acc,
    ml,
    col_own,
    col_prev,
    col_next,
    stats,
    inv_own,
    inv_prev,
    inv_next,
    out_buf,
    load_sem,
    small_sem,
    unit_send,
    unit_recv,
    relay_send,
    relay_recv,
    relay_b_send,
    relay_b_recv,
    q_send_sem,
    q_recv_sem,
    o_send_sem,
    o_recv_sem,
    ml_sem,
    stat_send,
    stat_recv,
    inv_sem,
    out_sem,
):
    heads, rows, _ = ql.shape
    tile = rows // 2
    model = heads * HEAD_DIM * group
    piece = tile // SUB
    chunks = 4 * heads * SUB
    via_two, via_one, via_zero, direct = routes(heads)
    s = lax.axis_index("seq")
    me = lax.axis_index("head")
    x = lax.rem(s, 4)
    first = s * 2

    def at(step):
        return {"seq": lax.rem(s + step + seqs, seqs), "head": me}

    def remote(src, dst, send, recv, where):
        return pltpu.make_async_remote_copy(
            src_ref=src, dst_ref=dst, send_sem=send, recv_sem=recv, device_id=where, device_id_type=MESH
        )

    barrier = pltpu.get_barrier_semaphore()

    def greet(where):
        pl.semaphore_signal(barrier, inc=1, device_id=where, device_id_type=MESH)

    greet(at(1))
    greet(at(-1))

    @pl.when((x == 0) | (x == 2))
    def _():
        greet(at(3))

    @pl.when((x == 1) | (x == 3))
    def _():
        greet(at(-3))

    @pl.when(x == 0)
    def _():
        greet(at(4))
        greet(at(-4))
        greet(at(-3))

    @pl.when(x == 1)
    def _():
        greet(at(3))

    for d in range(1, group):
        greet({"seq": s, "head": lax.rem(me + d, group)})

    def loads(which):
        src, dst = ((q_hbm, ql), (k_hbm, kl), (v_hbm, vl))[which]
        return [
            pltpu.make_async_copy(src.at[:, pl.ds(h * HEAD_DIM, HEAD_DIM)], dst.at[h], load_sem.at[which, h])
            for h in range(heads)
        ]

    small = [
        pltpu.make_async_copy(src, dst, small_sem.at[n])
        for n, (src, dst) in enumerate(
            ((qg_in, qg_ref), (kg_in, kg_ref), (tiles_in, tiles_ref), (count_in, count_ref))
        )
    ]
    for which in range(3):
        for copy in loads(which):
            copy.start()
    for copy in small:
        copy.start()

    ones = jnp.ones((8, HEAD_DIM), BF16)
    for which, buf in ((0, ql), (1, kl)):
        for copy in loads(which):
            copy.wait()

        def square_sum(h, total, buf=buf):
            wide = buf[h].astype(F32)
            return total + wide * wide

        left = lax.fori_loop(1, heads, square_sum, square_sum(0, 0.0))
        total = jnp.zeros((8, rows), F32)
        for _ in range(3):
            term = left.astype(BF16)
            total = total + dot_nt(ones, term)
            left = left - term.astype(F32)
        stats[me, :, which * rows : (which + 1) * rows] = total[:1]

    for copy in loads(2) + small:
        copy.wait()

    @pl.when(x == 0)
    def _():
        pl.semaphore_wait(barrier, group - 1 + 6)

    @pl.when(x == 1)
    def _():
        pl.semaphore_wait(barrier, group - 1 + 4)

    @pl.when(x > 1)
    def _():
        pl.semaphore_wait(barrier, group - 1 + 3)

    def stat_copy(d):
        return remote(
            stats.at[me], stats.at[me], stat_send.at[d], stat_recv.at[me], {"seq": s, "head": lax.rem(me + d, group)}
        )

    for d in range(1, group):
        stat_copy(d).start()

    def chunk_src(c):
        h, part, sub = c // (4 * SUB), (c // SUB) % 4, c % SUB
        src = vl if part % 2 else kl
        return src.at[h, pl.ds((0 if part >= 2 else tile) + sub * piece, piece)]

    def near_copies(h):
        return [
            remote(
                src.at[h, pl.ds(tile + sub * piece, piece)],
                halo.at[4 * SUB * h + part * SUB + sub],
                unit_send.at[4 * SUB * h + part * SUB + sub],
                unit_recv.at[4 * SUB * h + part * SUB + sub],
                at(1),
            )
            for part, src in ((0, kl), (1, vl))
            for sub in range(SUB)
        ]

    def far_copy(c):
        if c in via_two:
            i = via_two.index(c)
            return remote(chunk_src(c), relay_buf.at[i], unit_send.at[c], relay_recv.at[i], at(-1))
        if c in via_one:
            i = via_one.index(c)
            return remote(chunk_src(c), relay_b.at[i], unit_send.at[c], relay_b_recv.at[i], at(-1))
        if c in via_zero:
            i = via_zero.index(c)
            return remote(chunk_src(c), relay_buf.at[i], unit_send.at[c], relay_recv.at[i], at(-3))
        return remote(chunk_src(c), halo.at[c], unit_send.at[c], unit_recv.at[c], at(1))

    def q_copy(h):
        return remote(ql.at[h, pl.ds(0, tile)], q_next.at[h], q_send_sem.at[h], q_recv_sem.at[h], at(-1))

    early = sorted(via_one[:FAR_EARLY] + via_two[:FAR_EARLY] + via_zero[:FAR_EARLY])
    relayed = [c for c in sorted(via_one + via_two + via_zero) if c not in early]
    late, waiting = [], list(direct)
    while relayed or waiting:
        late, waiting = late + waiting[:1], waiting[1:]
        late, relayed = late + relayed[:PER_DIRECT], relayed[PER_DIRECT:]
    near_early = min(NEAR_EARLY, heads)

    @pl.when(x == 3)
    def _():
        for c in early:
            far_copy(c).start()
        q_copy(0).start()

    def near_start(h):
        for half in range(2):

            @pl.when(x < 3)
            def _(half=half):
                for copy in near_copies(h)[half * SUB : (half + 1) * SUB]:
                    copy.start()

            if half == 0:

                @pl.when((x > 0) & (x < 3))
                def _():
                    q_copy(h).start()

    for h in range(near_early):
        near_start(h)

    def relay_copy(i, at_x):
        if at_x == 0:
            return remote(relay_buf.at[i], halo.at[zero_slot(i)], relay_send.at[i], unit_recv.at[zero_slot(i)], at(4))
        if at_x == 1:
            return remote(relay_buf.at[i], halo.at[two_slot(i)], relay_send.at[i], unit_recv.at[two_slot(i)], at(-1))
        return remote(relay_buf.at[i], relay_buf.at[i], relay_send.at[i], relay_recv.at[i], at(3))

    def relay_count(at_x):
        return len(via_zero) if at_x == 0 else len(via_two)

    def relay(i, places):
        for at_x in places:

            @pl.when((x == at_x) & (i < relay_count(at_x)))
            def _(at_x=at_x):
                remote(relay_buf.at[i], relay_buf.at[i], relay_send.at[i], relay_recv.at[i], at(3)).wait_recv()
                relay_copy(i, at_x).start()

    def relay_b_copy(i, at_x):
        if at_x == 1:
            c = one_slot(i)
            return remote(relay_b.at[i], halo.at[c], relay_b_send.at[i], unit_recv.at[c], at(3))
        return remote(relay_b.at[i], relay_b.at[i], relay_b_send.at[i], relay_b_recv.at[i], at(-1))

    def relay_one(i, at_x):
        @pl.when((x == at_x) & (i < len(via_one)))
        def _():
            remote(relay_b.at[i], relay_b.at[i], relay_b_send.at[i], relay_b_recv.at[i], at(-1)).wait_recv()
            relay_b_copy(i, at_x).start()

    for d in range(1, group):
        other = lax.rem(me + group - d, group)
        remote(stats.at[other], stats.at[other], stat_send.at[d], stat_recv.at[other], at(1)).wait_recv()
    inv_own[...] = lax.rsqrt(jnp.sum(stats[...], axis=0) / model + NORM_EPS)

    def inv_copy(side):
        dst = (inv_prev, inv_next)[side]
        return remote(inv_own, dst, inv_sem.at[side], inv_sem.at[2 + side], at((1, -1)[side]))

    inv_copy(0).start()

    @pl.when(x > 0)
    def _():
        inv_copy(1).start()

    @pl.when(x == 3)
    def _():
        for n, c in enumerate(late):
            far_copy(c).start()
            if n % Q_EVERY == 1 and n // Q_EVERY + 1 < heads:
                q_copy(n // Q_EVERY + 1).start()
        for h in range((len(late) - 2) // Q_EVERY + 2, heads):
            q_copy(h).start()

    def to_columns(row):
        return jnp.transpose(jnp.broadcast_to(row, (HEAD_DIM, row.shape[1])))

    def normed(values, column, gain):
        return (values.astype(F32) * column * gain).astype(BF16)

    def gain_row(ref, h):
        return ref[pl.ds(pl.multiple_of(h * HEAD_DIM, HEAD_DIM), HEAD_DIM)].reshape(1, HEAD_DIM)

    col_own[...] = to_columns(inv_own[...])

    def norm_own(h, carry):
        qn[h] = normed(ql[h], col_own[:rows], gain_row(qg_ref, h))
        kn[h] = normed(kl[h], col_own[rows:], gain_row(kg_ref, h))
        return carry

    lax.fori_loop(0, heads, norm_own, 0)

    def seen(h, t, back):
        target = t - back
        count = count_ref[h, t]
        hit = jnp.int32(0)
        for w in range(WIN):
            hit = hit + jnp.where((tiles_ref[h, w, t] == target) & (w < count), 1, 0)
        return jnp.where((hit > 0) & (target >= 0), 1.0, 0.0).astype(F32)

    def top(scores, flag):
        return jnp.max(scores, axis=0, keepdims=True) * flag + (1.0 - flag) * LOW

    def shift(peak, flag):
        return peak * flag + (1.0 - flag) * HIGH

    def exps(scores, shifted):
        return jnp.exp2((scores - shifted) * EXP_SCALE)

    def row_sum(values):
        return jnp.sum(values, axis=0, keepdims=True)

    def two_blocks(keys, values, queries, flag_lo, flag_hi):
        scores = dot_nt(keys, queries)
        s_lo, s_hi = scores[:tile], scores[tile:]
        m_lo = top(s_lo, flag_lo)
        m_hi = jnp.max(s_hi, axis=0, keepdims=True) if flag_hi is None else top(s_hi, flag_hi)
        peak = jnp.maximum(m_lo, m_hi)
        p_lo = exps(s_lo, shift(peak, flag_lo))
        p_hi = exps(s_hi, peak if flag_hi is None else shift(peak, flag_hi))
        total = row_sum(p_lo) + row_sum(p_hi)
        mixed = dot_tn(values[:tile], p_lo.astype(BF16)) + dot_tn(values[tile:], p_hi.astype(BF16))
        return peak, total, mixed

    def local(h, carry):
        keys, values = kn[h], vl[h]
        scores = dot_nt(keys[:tile], qn[h, :tile])
        peak = jnp.max(scores, axis=0, keepdims=True)
        probs = exps(scores, peak)
        ml[h, 0:1] = peak
        ml[h, 1:2] = row_sum(probs)
        acc[h, 0] = dot_tn(values[:tile], probs.astype(BF16))
        peak, total, mixed = two_blocks(keys, values, qn[h, tile:], seen(h, first + 1, 1), None)
        ml[h, 2:3] = peak
        ml[h, 3:4] = total
        acc[h, 1] = mixed
        return carry

    def o_copy(h):
        return remote(o_send.at[h], o_recv.at[h], o_send_sem.at[h], o_recv_sem.at[h], at(1))

    def ml_copy():
        return remote(ml_send, ml_recv, ml_sem.at[0], ml_sem.at[1], at(1))

    def for_next(h, carry):
        q_copy(h).wait_recv()
        queries = normed(q_next[h], col_next[...], gain_row(qg_ref, h))
        peak, total, mixed = two_blocks(
            kn[h], vl[h], queries, seen(h, first + 2, 2), seen(h, first + 2, 1)
        )
        ml_send[h, 0:1] = peak
        ml_send[h, 1:2] = total
        o_send[h] = mixed.astype(BF16)
        o_copy(h).start()
        return carry

    def local_step(h, carry):
        relay_one(h, 2)
        relay(h, (0, 2))

        @pl.when(h + near_early < heads)
        def _():
            near_start(h + near_early)

        return local(h, carry)

    lax.fori_loop(0, heads, local_step, 0)

    @pl.when(x < 3)
    def _():
        inv_copy(1).wait_recv()
        col_next[...] = to_columns(inv_next[:, :tile])

        def next_step(h, carry):
            relay_one(heads + h, 2)
            relay(heads + h, (0, 2))
            relay_one(h, 1)
            relay(h, (1,))
            return for_next(h, carry)

        lax.fori_loop(0, heads, next_step, 0)
        ml_copy().start()

    inv_copy(0).wait_recv()
    col_prev[...] = to_columns(inv_prev[:, rows:])

    def finish(h, part, total, mixed):
        out_buf[h, part * tile : (part + 1) * tile] = jnp.transpose(mixed * (1.0 / total)).astype(BF16)

    def out_copy(h):
        return pltpu.make_async_copy(
            out_buf.at[h], out_hbm.at[:, pl.ds(pl.multiple_of(h * HEAD_DIM, HEAD_DIM), HEAD_DIM)], out_sem.at[h]
        )

    def part_wait(h, part):
        for sub in range(SUB):
            c = (4 * h + part) * SUB + sub
            remote(halo.at[c], halo.at[c], unit_send.at[c], unit_recv.at[c], at(1)).wait_recv()

    def arrived(h, part):
        return halo[pl.ds((4 * h + part) * SUB, SUB)].reshape(tile, HEAD_DIM)

    def high_tile(h):
        keys = normed(arrived(h, 0), col_prev[tile:], gain_row(kg_ref, h))
        values = arrived(h, 1)
        flag = seen(h, first + 1, 2)
        scores = dot_nt(keys, qn[h, tile:])
        before = ml[h, 2:3]
        peak = jnp.maximum(before, top(scores, flag))
        probs = exps(scores, shift(peak, flag))
        fade = exps(before, peak)
        total = ml[h, 3:4] * fade + row_sum(probs)
        mixed = acc[h, 1] * fade + dot_tn(values, probs.astype(BF16))
        finish(h, 1, total, mixed)
        return keys

    def far_head(h):
        for part in range(4):
            part_wait(h, part)
        keys_hi = high_tile(h)
        keys_lo = normed(arrived(h, 2), col_prev[:tile], gain_row(kg_ref, h))
        keys = jnp.concatenate([keys_lo, keys_hi], axis=0)
        values = jnp.concatenate([arrived(h, 3), arrived(h, 1)], axis=0)
        peak_far, total_far, mixed_far = two_blocks(
            keys, values, qn[h, :tile], seen(h, first, 2), seen(h, first, 1)
        )
        merge(h, peak_far, total_far, mixed_far)

    def merge(h, peak_far, total_far, mixed_far):
        before = ml[h, 0:1]
        peak = jnp.maximum(before, peak_far)
        fade, fade_far = exps(before, peak), exps(peak_far, peak)
        finish(h, 0, ml[h, 1:2] * fade + total_far * fade_far, acc[h, 0] * fade + mixed_far * fade_far)
        out_copy(h).start()

    def near_high(h, carry):
        part_wait(h, 0)
        part_wait(h, 1)
        high_tile(h)
        return carry

    def near_low(h, carry):
        o_copy(h).wait_recv()
        merge(h, ml_recv[h, 0:1], ml_recv[h, 1:2], o_recv[h].astype(F32))
        return carry

    def loop(lo, hi, body):
        lax.fori_loop(lo, hi, lambda h, c: body(h, c), 0)

    def relays(lo, hi, at_x):
        loop(lo, hi, lambda i, c: (relay(i, (at_x,)), c)[1])

    @pl.when(x == 0)
    def _():
        tail = len(via_zero) - 2 * heads

        relays(2 * heads, 2 * heads + tail - FAR_AHEAD, 0)

        def step(h, carry):
            relay(2 * heads + tail - FAR_AHEAD + h, (0,))
            far_head(h)
            return carry

        loop(0, heads, step)

    @pl.when(x == 1)
    def _():
        def step(h, carry):
            relay_one(heads + h, 1)
            relay(heads + h, (1,))
            return near_high(h, carry)

        loop(0, heads, step)
        relays(2 * heads, len(via_two), 1)

    @pl.when(x == 2)
    def _():
        relays(2 * heads, len(via_two), 2)
        loop(0, heads, near_high)

    @pl.when(x == 3)
    def _():
        loop(0, heads, near_high)

    @pl.when(x > 0)
    def _():
        ml_copy().wait_recv()
        loop(0, heads, near_low)

    for h in range(heads):
        out_copy(h).wait()
    for d in range(1, group):
        stat_copy(d).wait_send()
    inv_copy(0).wait_send()

    @pl.when(x > 0)
    def _():
        inv_copy(1).wait_send()
        for h in range(heads):
            q_copy(h).wait_send()

    @pl.when(x == 3)
    def _():
        for c in range(chunks):
            far_copy(c).wait_send()

    @pl.when(x < 3)
    def _():
        for h in range(heads):
            for copy in near_copies(h):
                copy.wait_send()
            o_copy(h).wait_send()
        ml_copy().wait_send()

    for at_x in range(3):

        @pl.when(x == at_x)
        def _(at_x=at_x):
            for i in range(relay_count(at_x)):
                relay_copy(i, at_x).wait_send()
            if at_x > 0:
                for i in range(len(via_one)):
                    relay_b_copy(i, at_x).wait_send()


def per_device(q_proj, k_proj, v_proj, q_gain, k_gain, window_tiles, window_count):
    seqs, group = lax.axis_size("seq"), lax.axis_size("head")
    rows, cols = q_proj.shape
    heads, tile = cols // HEAD_DIM, rows // 2
    chunks = 4 * heads * SUB
    via_two, via_one, via_zero, _ = routes(heads)
    slots = max(len(via_two), len(via_zero))
    slots_b = len(via_one)
    dma = pltpu.SemaphoreType.DMA
    anywhere = pl.BlockSpec(memory_space=pl.ANY)
    hbm = pl.BlockSpec(memory_space=pltpu.HBM)
    flops = 30 * heads * tile * tile * HEAD_DIM
    return pl.pallas_call(
        functools.partial(kernel, seqs, group),
        out_shape=jax.ShapeDtypeStruct((rows, cols), BF16),
        in_specs=[hbm] * 7,
        out_specs=anywhere,
        scratch_shapes=[
            pltpu.VMEM(q_gain.shape, F32),
            pltpu.VMEM(k_gain.shape, F32),
            pltpu.SMEM((heads, WIN, window_count.shape[1]), jnp.int32),
            pltpu.SMEM(window_count.shape, jnp.int32),
            pltpu.VMEM((heads, rows, HEAD_DIM), BF16),
            pltpu.VMEM((heads, rows, HEAD_DIM), BF16),
            pltpu.VMEM((heads, rows, HEAD_DIM), BF16),
            pltpu.VMEM((heads, rows, HEAD_DIM), BF16),
            pltpu.VMEM((heads, rows, HEAD_DIM), BF16),
            pltpu.VMEM((chunks, tile // SUB, HEAD_DIM), BF16),
            pltpu.VMEM((slots, tile // SUB, HEAD_DIM), BF16),
            pltpu.VMEM((slots_b, tile // SUB, HEAD_DIM), BF16),
            pltpu.VMEM((heads, tile, HEAD_DIM), BF16),
            pltpu.VMEM((heads, HEAD_DIM, tile), BF16),
            pltpu.VMEM((heads, HEAD_DIM, tile), BF16),
            pltpu.VMEM((heads, 2, tile), F32),
            pltpu.VMEM((heads, 2, tile), F32),
            pltpu.VMEM((heads, 2, HEAD_DIM, tile), F32),
            pltpu.VMEM((heads, 4, tile), F32),
            pltpu.VMEM((2 * rows, HEAD_DIM), F32),
            pltpu.VMEM((rows, HEAD_DIM), F32),
            pltpu.VMEM((tile, HEAD_DIM), F32),
            pltpu.VMEM((group, 1, 2 * rows), F32),
            pltpu.VMEM((1, 2 * rows), F32),
            pltpu.VMEM((1, 2 * rows), F32),
            pltpu.VMEM((1, 2 * rows), F32),
            pltpu.VMEM((heads, rows, HEAD_DIM), BF16),
            dma((3, heads)),
            dma((4,)),
            dma((chunks,)),
            dma((chunks,)),
            dma((slots,)),
            dma((slots,)),
            dma((slots_b,)),
            dma((slots_b,)),
            dma((heads,)),
            dma((heads,)),
            dma((heads,)),
            dma((heads,)),
            dma((2,)),
            dma((group,)),
            dma((group,)),
            dma((4,)),
            dma((heads,)),
        ],
        compiler_params=pltpu.CompilerParams(
            collective_id=0, has_side_effects=True, vmem_limit_bytes=48 * 1024 * 1024
        ),
        cost_estimate=pl.CostEstimate(flops=flops, bytes_accessed=4 * rows * cols * 2, transcendentals=0),
        name="window_attention",
    )(
        *(
            pltpu.with_memory_space_constraint(a, pltpu.HBM)
            for a in (q_proj, k_proj, v_proj, q_gain, k_gain, window_tiles.transpose(0, 2, 1), window_count)
        )
    )


def solution(mesh):
    return jax.shard_map(
        per_device,
        mesh=mesh,
        in_specs=(
            P("seq", "head"),
            P("seq", "head"),
            P("seq", "head"),
            P("head"),
            P("head"),
            P("head", None, None),
            P("head", None),
        ),
        out_specs=P("seq", "head"),
        check_vma=False,
    )
```

```python
import functools
import math

import jax
import jax.numpy as jnp
from jax import lax
from jax.experimental import pallas as pl
from jax.experimental.pallas import tpu as pltpu
from jax.sharding import PartitionSpec as P

HEAD_DIM = 128
WIN = 3
NORM_EPS = 1e-06
EXP_SCALE = math.log2(math.e) / math.sqrt(HEAD_DIM)
LOW = -1e30
HIGH = 1e30
F32 = jnp.float32
BF16 = jnp.bfloat16
MESH = pl.DeviceIdType.MESH


def dot_nt(a, b):
    return lax.dot_general(a, b, (((1,), (1,)), ((), ())), preferred_element_type=F32)


def dot_tn(a, b):
    return lax.dot_general(a, b, (((0,), (0,)), ((), ())), preferred_element_type=F32)


SUB = 2
FAR_EARLY = 4
FAR_AHEAD = 1
PER_DIRECT = 10
Q_EVERY = 7
NEAR_EARLY = 2


def two_slot(i):
    return 10 * (i // 2) + 6 * (i % 2)


def one_slot(i):
    return two_slot(i) + 1


def zero_slot(i):
    return 10 * (i // 3) + 3 * (i % 3) + 2


def routes(heads):
    chunks = 4 * heads * SUB
    via_two, via_one, via_zero = (
        [slot(i) for i in range(chunks) if slot(i) < chunks] for slot in (two_slot, one_slot, zero_slot)
    )
    direct = [c for c in range(chunks) if c not in via_two + via_one + via_zero]
    return via_two, via_one, via_zero, direct


def kernel(
    seqs,
    group,
    q_hbm,
    k_hbm,
    v_hbm,
    qg_in,
    kg_in,
    tiles_in,
    count_in,
    out_hbm,
    qg_ref,
    kg_ref,
    tiles_ref,
    count_ref,
    ql,
    kl,
    vl,
    qn,
    kn,
    halo,
    relay_buf,
    relay_b,
    q_next,
    o_send,
    o_recv,
    ml_send,
    ml_recv,
    acc,
    ml,
    col_own,
    col_prev,
    col_next,
    stats,
    inv_own,
    inv_prev,
    inv_next,
    out_buf,
    load_sem,
    small_sem,
    unit_send,
    unit_recv,
    relay_send,
    relay_recv,
    relay_b_send,
    relay_b_recv,
    q_send_sem,
    q_recv_sem,
    o_send_sem,
    o_recv_sem,
    ml_sem,
    stat_send,
    stat_recv,
    inv_sem,
    out_sem,
):
    heads, rows, _ = ql.shape
    tile = rows // 2
    model = heads * HEAD_DIM * group
    piece = tile // SUB
    chunks = 4 * heads * SUB
    via_two, via_one, via_zero, direct = routes(heads)
    s = lax.axis_index("seq")
    me = lax.axis_index("head")
    x = lax.rem(s, 4)
    first = s * 2

    def at(step):
        return {"seq": lax.rem(s + step + seqs, seqs), "head": me}

    def remote(src, dst, send, recv, where):
        return pltpu.make_async_remote_copy(
            src_ref=src, dst_ref=dst, send_sem=send, recv_sem=recv, device_id=where, device_id_type=MESH
        )

    barrier = pltpu.get_barrier_semaphore()

    def greet(where):
        pl.semaphore_signal(barrier, inc=1, device_id=where, device_id_type=MESH)

    greet(at(1))
    greet(at(-1))

    @pl.when((x == 0) | (x == 2))
    def _():
        greet(at(3))

    @pl.when((x == 1) | (x == 3))
    def _():
        greet(at(-3))

    @pl.when(x == 0)
    def _():
        greet(at(4))
        greet(at(-4))
        greet(at(-3))

    @pl.when(x == 1)
    def _():
        greet(at(3))

    for d in range(1, group):
        greet({"seq": s, "head": lax.rem(me + d, group)})

    def loads(which):
        src, dst = ((q_hbm, ql), (k_hbm, kl), (v_hbm, vl))[which]
        return [
            pltpu.make_async_copy(src.at[:, pl.ds(h * HEAD_DIM, HEAD_DIM)], dst.at[h], load_sem.at[which, h])
            for h in range(heads)
        ]

    small = [
        pltpu.make_async_copy(src, dst, small_sem.at[n])
        for n, (src, dst) in enumerate(
            ((qg_in, qg_ref), (kg_in, kg_ref), (tiles_in, tiles_ref), (count_in, count_ref))
        )
    ]
    for which in range(3):
        for copy in loads(which):
            copy.start()
    for copy in small:
        copy.start()

    ones = jnp.ones((8, HEAD_DIM), BF16)
    for which, buf in ((0, ql), (1, kl)):
        for copy in loads(which):
            copy.wait()

        def square_sum(h, total, buf=buf):
            wide = buf[h].astype(F32)
            return total + wide * wide

        left = lax.fori_loop(1, heads, square_sum, square_sum(0, 0.0))
        total = jnp.zeros((8, rows), F32)
        for _ in range(3):
            term = left.astype(BF16)
            total = total + dot_nt(ones, term)
            left = left - term.astype(F32)
        stats[me, :, which * rows : (which + 1) * rows] = total[:1]

    for copy in loads(2) + small:
        copy.wait()

    @pl.when(x == 0)
    def _():
        pl.semaphore_wait(barrier, group - 1 + 6)

    @pl.when(x == 1)
    def _():
        pl.semaphore_wait(barrier, group - 1 + 4)

    @pl.when(x > 1)
    def _():
        pl.semaphore_wait(barrier, group - 1 + 3)

    def stat_copy(d):
        return remote(
            stats.at[me], stats.at[me], stat_send.at[d], stat_recv.at[me], {"seq": s, "head": lax.rem(me + d, group)}
        )

    for d in range(1, group):
        stat_copy(d).start()

    def chunk_src(c):
        h, part, sub = c // (4 * SUB), (c // SUB) % 4, c % SUB
        src = vl if part % 2 else kl
        return src.at[h, pl.ds((0 if part >= 2 else tile) + sub * piece, piece)]

    def near_copies(h):
        return [
            remote(
                src.at[h, pl.ds(tile + sub * piece, piece)],
                halo.at[4 * SUB * h + part * SUB + sub],
                unit_send.at[4 * SUB * h + part * SUB + sub],
                unit_recv.at[4 * SUB * h + part * SUB + sub],
                at(1),
            )
            for part, src in ((0, kl), (1, vl))
            for sub in range(SUB)
        ]

    def far_copy(c):
        if c in via_two:
            i = via_two.index(c)
            return remote(chunk_src(c), relay_buf.at[i], unit_send.at[c], relay_recv.at[i], at(-1))
        if c in via_one:
            i = via_one.index(c)
            return remote(chunk_src(c), relay_b.at[i], unit_send.at[c], relay_b_recv.at[i], at(-1))
        if c in via_zero:
            i = via_zero.index(c)
            return remote(chunk_src(c), relay_buf.at[i], unit_send.at[c], relay_recv.at[i], at(-3))
        return remote(chunk_src(c), halo.at[c], unit_send.at[c], unit_recv.at[c], at(1))

    def q_copy(h):
        return remote(ql.at[h, pl.ds(0, tile)], q_next.at[h], q_send_sem.at[h], q_recv_sem.at[h], at(-1))

    early = sorted(via_one[:FAR_EARLY] + via_two[:FAR_EARLY] + via_zero[:FAR_EARLY])
    relayed = [c for c in sorted(via_one + via_two + via_zero) if c not in early]
    late, waiting = [], list(direct)
    while relayed or waiting:
        late, waiting = late + waiting[:1], waiting[1:]
        late, relayed = late + relayed[:PER_DIRECT], relayed[PER_DIRECT:]
    near_early = min(NEAR_EARLY, heads)

    @pl.when(x == 3)
    def _():
        for c in early:
            far_copy(c).start()
        q_copy(0).start()

    def near_start(h):
        for half in range(2):

            @pl.when(x < 3)
            def _(half=half):
                for copy in near_copies(h)[half * SUB : (half + 1) * SUB]:
                    copy.start()

            if half == 0:

                @pl.when((x > 0) & (x < 3))
                def _():
                    q_copy(h).start()

    for h in range(near_early):
        near_start(h)

    def relay_copy(i, at_x):
        if at_x == 0:
            return remote(relay_buf.at[i], halo.at[zero_slot(i)], relay_send.at[i], unit_recv.at[zero_slot(i)], at(4))
        if at_x == 1:
            return remote(relay_buf.at[i], halo.at[two_slot(i)], relay_send.at[i], unit_recv.at[two_slot(i)], at(-1))
        return remote(relay_buf.at[i], relay_buf.at[i], relay_send.at[i], relay_recv.at[i], at(3))

    def relay_count(at_x):
        return len(via_zero) if at_x == 0 else len(via_two)

    def relay(i, places):
        for at_x in places:

            @pl.when((x == at_x) & (i < relay_count(at_x)))
            def _(at_x=at_x):
                remote(relay_buf.at[i], relay_buf.at[i], relay_send.at[i], relay_recv.at[i], at(3)).wait_recv()
                relay_copy(i, at_x).start()

    def relay_b_copy(i, at_x):
        if at_x == 1:
            c = one_slot(i)
            return remote(relay_b.at[i], halo.at[c], relay_b_send.at[i], unit_recv.at[c], at(3))
        return remote(relay_b.at[i], relay_b.at[i], relay_b_send.at[i], relay_b_recv.at[i], at(-1))

    def relay_one(i, at_x):
        @pl.when((x == at_x) & (i < len(via_one)))
        def _():
            remote(relay_b.at[i], relay_b.at[i], relay_b_send.at[i], relay_b_recv.at[i], at(-1)).wait_recv()
            relay_b_copy(i, at_x).start()

    for d in range(1, group):
        other = lax.rem(me + group - d, group)
        remote(stats.at[other], stats.at[other], stat_send.at[d], stat_recv.at[other], at(1)).wait_recv()
    inv_own[...] = lax.rsqrt(jnp.sum(stats[...], axis=0) / model + NORM_EPS)

    def inv_copy(side):
        dst = (inv_prev, inv_next)[side]
        return remote(inv_own, dst, inv_sem.at[side], inv_sem.at[2 + side], at((1, -1)[side]))

    inv_copy(0).start()

    @pl.when(x > 0)
    def _():
        inv_copy(1).start()

    @pl.when(x == 3)
    def _():
        for n, c in enumerate(late):
            far_copy(c).start()
            if n % Q_EVERY == 1 and n // Q_EVERY + 1 < heads:
                q_copy(n // Q_EVERY + 1).start()
        for h in range((len(late) - 2) // Q_EVERY + 2, heads):
            q_copy(h).start()

    def to_columns(row):
        return jnp.transpose(jnp.broadcast_to(row, (HEAD_DIM, row.shape[1])))

    def normed(values, column, gain):
        return (values.astype(F32) * column * gain).astype(BF16)

    def gain_row(ref, h):
        return ref[pl.ds(pl.multiple_of(h * HEAD_DIM, HEAD_DIM), HEAD_DIM)].reshape(1, HEAD_DIM)

    col_own[...] = to_columns(inv_own[...])

    def norm_own(h, carry):
        qn[h] = normed(ql[h], col_own[:rows], gain_row(qg_ref, h))
        kn[h] = normed(kl[h], col_own[rows:], gain_row(kg_ref, h))
        return carry

    lax.fori_loop(0, heads, norm_own, 0)

    def seen(h, t, back):
        target = t - back
        count = count_ref[h, t]
        hit = jnp.int32(0)
        for w in range(WIN):
            hit = hit + jnp.where((tiles_ref[h, w, t] == target) & (w < count), 1, 0)
        return jnp.where((hit > 0) & (target >= 0), 1.0, 0.0).astype(F32)

    def top(scores, flag):
        return jnp.max(scores, axis=0, keepdims=True) * flag + (1.0 - flag) * LOW

    def shift(peak, flag):
        return peak * flag + (1.0 - flag) * HIGH

    def exps(scores, shifted):
        return jnp.exp2((scores - shifted) * EXP_SCALE)

    def row_sum(values):
        return jnp.sum(values, axis=0, keepdims=True)

    def two_blocks(keys, values, queries, flag_lo, flag_hi):
        scores = dot_nt(keys, queries)
        s_lo, s_hi = scores[:tile], scores[tile:]
        m_lo = top(s_lo, flag_lo)
        m_hi = jnp.max(s_hi, axis=0, keepdims=True) if flag_hi is None else top(s_hi, flag_hi)
        peak = jnp.maximum(m_lo, m_hi)
        p_lo = exps(s_lo, shift(peak, flag_lo))
        p_hi = exps(s_hi, peak if flag_hi is None else shift(peak, flag_hi))
        total = row_sum(p_lo) + row_sum(p_hi)
        mixed = dot_tn(values[:tile], p_lo.astype(BF16)) + dot_tn(values[tile:], p_hi.astype(BF16))
        return peak, total, mixed

    def local(h, carry):
        keys, values = kn[h], vl[h]
        scores = dot_nt(keys[:tile], qn[h, :tile])
        peak = jnp.max(scores, axis=0, keepdims=True)
        probs = exps(scores, peak)
        ml[h, 0:1] = peak
        ml[h, 1:2] = row_sum(probs)
        acc[h, 0] = dot_tn(values[:tile], probs.astype(BF16))
        peak, total, mixed = two_blocks(keys, values, qn[h, tile:], seen(h, first + 1, 1), None)
        ml[h, 2:3] = peak
        ml[h, 3:4] = total
        acc[h, 1] = mixed
        return carry

    def o_copy(h):
        return remote(o_send.at[h], o_recv.at[h], o_send_sem.at[h], o_recv_sem.at[h], at(1))

    def ml_copy():
        return remote(ml_send, ml_recv, ml_sem.at[0], ml_sem.at[1], at(1))

    def for_next(h, carry):
        q_copy(h).wait_recv()
        queries = normed(q_next[h], col_next[...], gain_row(qg_ref, h))
        peak, total, mixed = two_blocks(
            kn[h], vl[h], queries, seen(h, first + 2, 2), seen(h, first + 2, 1)
        )
        ml_send[h, 0:1] = peak
        ml_send[h, 1:2] = total
        o_send[h] = mixed.astype(BF16)
        o_copy(h).start()
        return carry

    def local_step(h, carry):
        relay_one(h, 2)
        relay(h, (0, 2))

        @pl.when(h + near_early < heads)
        def _():
            near_start(h + near_early)

        return local(h, carry)

    lax.fori_loop(0, heads, local_step, 0)

    @pl.when(x < 3)
    def _():
        inv_copy(1).wait_recv()
        col_next[...] = to_columns(inv_next[:, :tile])

        def next_step(h, carry):
            relay_one(heads + h, 2)
            relay(heads + h, (0, 2))
            relay_one(h, 1)
            relay(h, (1,))
            return for_next(h, carry)

        lax.fori_loop(0, heads, next_step, 0)
        ml_copy().start()

    inv_copy(0).wait_recv()
    col_prev[...] = to_columns(inv_prev[:, rows:])

    def finish(h, part, total, mixed):
        out_buf[h, part * tile : (part + 1) * tile] = jnp.transpose(mixed * (1.0 / total)).astype(BF16)

    def out_copy(h):
        return pltpu.make_async_copy(
            out_buf.at[h], out_hbm.at[:, pl.ds(pl.multiple_of(h * HEAD_DIM, HEAD_DIM), HEAD_DIM)], out_sem.at[h]
        )

    def part_wait(h, part):
        for sub in range(SUB):
            c = (4 * h + part) * SUB + sub
            remote(halo.at[c], halo.at[c], unit_send.at[c], unit_recv.at[c], at(1)).wait_recv()

    def arrived(h, part):
        return halo[pl.ds((4 * h + part) * SUB, SUB)].reshape(tile, HEAD_DIM)

    def high_tile(h):
        keys = normed(arrived(h, 0), col_prev[tile:], gain_row(kg_ref, h))
        values = arrived(h, 1)
        flag = seen(h, first + 1, 2)
        scores = dot_nt(keys, qn[h, tile:])
        before = ml[h, 2:3]
        peak = jnp.maximum(before, top(scores, flag))
        probs = exps(scores, shift(peak, flag))
        fade = exps(before, peak)
        total = ml[h, 3:4] * fade + row_sum(probs)
        mixed = acc[h, 1] * fade + dot_tn(values, probs.astype(BF16))
        finish(h, 1, total, mixed)
        return keys

    def far_head(h):
        for part in range(4):
            part_wait(h, part)
        keys_hi = high_tile(h)
        keys_lo = normed(arrived(h, 2), col_prev[:tile], gain_row(kg_ref, h))
        keys = jnp.concatenate([keys_lo, keys_hi], axis=0)
        values = jnp.concatenate([arrived(h, 3), arrived(h, 1)], axis=0)
        peak_far, total_far, mixed_far = two_blocks(
            keys, values, qn[h, :tile], seen(h, first, 2), seen(h, first, 1)
        )
        merge(h, peak_far, total_far, mixed_far)

    def merge(h, peak_far, total_far, mixed_far):
        before = ml[h, 0:1]
        peak = jnp.maximum(before, peak_far)
        fade, fade_far = exps(before, peak), exps(peak_far, peak)
        finish(h, 0, ml[h, 1:2] * fade + total_far * fade_far, acc[h, 0] * fade + mixed_far * fade_far)
        out_copy(h).start()

    def near_high(h, carry):
        part_wait(h, 0)
        part_wait(h, 1)
        high_tile(h)
        return carry

    def near_low(h, carry):
        o_copy(h).wait_recv()
        merge(h, ml_recv[h, 0:1], ml_recv[h, 1:2], o_recv[h].astype(F32))
        return carry

    def loop(lo, hi, body):
        lax.fori_loop(lo, hi, lambda h, c: body(h, c), 0)

    def relays(lo, hi, at_x):
        loop(lo, hi, lambda i, c: (relay(i, (at_x,)), c)[1])

    @pl.when(x == 0)
    def _():
        tail = len(via_zero) - 2 * heads

        relays(2 * heads, 2 * heads + tail - FAR_AHEAD, 0)

        def step(h, carry):
            relay(2 * heads + tail - FAR_AHEAD + h, (0,))
            far_head(h)
            return carry

        loop(0, heads, step)

    @pl.when(x == 1)
    def _():
        def step(h, carry):
            relay_one(heads + h, 1)
            relay(heads + h, (1,))
            return near_high(h, carry)

        loop(0, heads, step)
        relays(2 * heads, len(via_two), 1)

    @pl.when(x == 2)
    def _():
        relays(2 * heads, len(via_two), 2)
        loop(0, heads, near_high)

    @pl.when(x == 3)
    def _():
        loop(0, heads, near_high)

    @pl.when(x > 0)
    def _():
        ml_copy().wait_recv()
        loop(0, heads, near_low)

    for h in range(heads):
        out_copy(h).wait()
    for d in range(1, group):
        stat_copy(d).wait_send()
    inv_copy(0).wait_send()

    @pl.when(x > 0)
    def _():
        inv_copy(1).wait_send()
        for h in range(heads):
            q_copy(h).wait_send()

    @pl.when(x == 3)
    def _():
        for c in range(chunks):
            far_copy(c).wait_send()

    @pl.when(x < 3)
    def _():
        for h in range(heads):
            for copy in near_copies(h):
                copy.wait_send()
            o_copy(h).wait_send()
        ml_copy().wait_send()

    for at_x in range(3):

        @pl.when(x == at_x)
        def _(at_x=at_x):
            for i in range(relay_count(at_x)):
                relay_copy(i, at_x).wait_send()
            if at_x > 0:
                for i in range(len(via_one)):
                    relay_b_copy(i, at_x).wait_send()


def per_device(q_proj, k_proj, v_proj, q_gain, k_gain, window_tiles, window_count):
    seqs, group = lax.axis_size("seq"), lax.axis_size("head")
    rows, cols = q_proj.shape
    heads, tile = cols // HEAD_DIM, rows // 2
    chunks = 4 * heads * SUB
    via_two, via_one, via_zero, _ = routes(heads)
    slots = max(len(via_two), len(via_zero))
    slots_b = len(via_one)
    dma = pltpu.SemaphoreType.DMA
    anywhere = pl.BlockSpec(memory_space=pl.ANY)
    hbm = pl.BlockSpec(memory_space=pltpu.HBM)
    flops = 30 * heads * tile * tile * HEAD_DIM
    return pl.pallas_call(
        functools.partial(kernel, seqs, group),
        out_shape=jax.ShapeDtypeStruct((rows, cols), BF16),
        in_specs=[hbm] * 7,
        out_specs=anywhere,
        scratch_shapes=[
            pltpu.VMEM(q_gain.shape, F32),
            pltpu.VMEM(k_gain.shape, F32),
            pltpu.SMEM((heads, WIN, window_count.shape[1]), jnp.int32),
            pltpu.SMEM(window_count.shape, jnp.int32),
            pltpu.VMEM((heads, rows, HEAD_DIM), BF16),
            pltpu.VMEM((heads, rows, HEAD_DIM), BF16),
            pltpu.VMEM((heads, rows, HEAD_DIM), BF16),
            pltpu.VMEM((heads, rows, HEAD_DIM), BF16),
            pltpu.VMEM((heads, rows, HEAD_DIM), BF16),
            pltpu.VMEM((chunks, tile // SUB, HEAD_DIM), BF16),
            pltpu.VMEM((slots, tile // SUB, HEAD_DIM), BF16),
            pltpu.VMEM((slots_b, tile // SUB, HEAD_DIM), BF16),
            pltpu.VMEM((heads, tile, HEAD_DIM), BF16),
            pltpu.VMEM((heads, HEAD_DIM, tile), BF16),
            pltpu.VMEM((heads, HEAD_DIM, tile), BF16),
            pltpu.VMEM((heads, 2, tile), F32),
            pltpu.VMEM((heads, 2, tile), F32),
            pltpu.VMEM((heads, 2, HEAD_DIM, tile), F32),
            pltpu.VMEM((heads, 4, tile), F32),
            pltpu.VMEM((2 * rows, HEAD_DIM), F32),
            pltpu.VMEM((rows, HEAD_DIM), F32),
            pltpu.VMEM((tile, HEAD_DIM), F32),
            pltpu.VMEM((group, 1, 2 * rows), F32),
            pltpu.VMEM((1, 2 * rows), F32),
            pltpu.VMEM((1, 2 * rows), F32),
            pltpu.VMEM((1, 2 * rows), F32),
            pltpu.VMEM((heads, rows, HEAD_DIM), BF16),
            dma((3, heads)),
            dma((4,)),
            dma((chunks,)),
            dma((chunks,)),
            dma((slots,)),
            dma((slots,)),
            dma((slots_b,)),
            dma((slots_b,)),
            dma((heads,)),
            dma((heads,)),
            dma((heads,)),
            dma((heads,)),
            dma((2,)),
            dma((group,)),
            dma((group,)),
            dma((4,)),
            dma((heads,)),
        ],
        compiler_params=pltpu.CompilerParams(
            collective_id=0, has_side_effects=True, vmem_limit_bytes=48 * 1024 * 1024
        ),
        cost_estimate=pl.CostEstimate(flops=flops, bytes_accessed=4 * rows * cols * 2, transcendentals=0),
        name="window_attention",
    )(
        *(
            pltpu.with_memory_space_constraint(a, pltpu.HBM)
            for a in (q_proj, k_proj, v_proj, q_gain, k_gain, window_tiles.transpose(0, 2, 1), window_count)
        )
    )


def solution(mesh):
    return jax.shard_map(
        per_device,
        mesh=mesh,
        in_specs=(
            P("seq", "head"),
            P("seq", "head"),
            P("seq", "head"),
            P("head"),
            P("head"),
            P("head", None, None),
            P("head", None),
        ),
        out_specs=P("seq", "head"),
        check_vma=False,
    )
```
